32 devices in a mesh: gx: 8 (over z, y), gy: 4 (over x, core).
Axes of the slice: x: 2, y: 2, z: 4, core: 2. Of those that a mesh axis runs over, the one named last changes fastest.
Arguments:
- latents: bfloat16 [8, 4, 512, 128], P('gx', 'gy'), may hold values from -6 to 6
- edge_latents: bfloat16 [8, 4, 4096, 128], P('gx', 'gy'), may hold values from -6 to 6
- senders: int32 [8, 4, 4096], P('gx', 'gy'), may hold values from 0 to 1663, as said below
- receivers: int32 [8, 4, 4096], P('gx', 'gy'), may hold values from 0 to 255
- ghost_rows: int32 [8, 4, 3, 3, 128], P('gx', 'gy'), may hold values from 0 to 511
- edge_count: int32 [8, 4], P('gx', 'gy'), may hold values from 1024 to 4096, as said below
- node_cotangent: bfloat16 [8, 4, 512, 128], P('gx', 'gy'), may hold values from -6 to 6
- edge_cotangent: bfloat16 [8, 4, 4096, 128], P('gx', 'gy'), may hold values from -6 to 6
- edge_first: bfloat16 [2, 384, 128], replicated, may hold values from -0.3125 to 0.3125
- edge_second: bfloat16 [2, 128, 128], replicated, may hold values from -0.5 to 0.5
- edge_scale: float32 [2, 128], replicated, may hold values from 0.5 to 1.5
- node_first: bfloat16 [2, 256, 128], replicated, may hold values from -0.375 to 0.375
- node_second: bfloat16 [2, 128, 128], replicated, may hold values from -0.5 to 0.5
- node_scale: float32 [2, 128], replicated, may hold values from 0.5 to 1.5
Outputs:
- nodes_out: bfloat16 [8, 4, 512, 128], P('gx', 'gy')
- edges_out: bfloat16 [8, 4, 4096, 128], P('gx', 'gy')
- latents_grad: float32 [8, 4, 512, 128], P('gx', 'gy')
- edge_latents_grad: float32 [8, 4, 4096, 128], P('gx', 'gy')
- edge_first_grad: float32 [2, 384, 128], replicated
- edge_second_grad: float32 [2, 128, 128], replicated
- edge_scale_grad: float32 [2, 128], replicated
- node_first_grad: float32 [2, 256, 128], replicated
- node_second_grad: float32 [2, 128, 128], replicated
- node_scale_grad: float32 [2, 128], replicated
The draws below stay inside these ranges and needn't reach their ends.
Inputs may be any that keep to these rules, and one draw needn't show every extreme that they name: `senders`: rows 0 to 511 of the node table are the domain's particles; row 512 + k * 128 + j is ghost row j of slot k = 3 a + b, from the neighbour at offset (a - 1, b - 1); slot 4 is never named. `edge_count`: edge slots at positions below the count are live, later ones are padding.
All inputs are finite; a program needn't handle non-finite values.
Results may differ from the reference program's by a relative error of at most 0.02.
Values may be sent and summed in bfloat16 or wider, within the bound.
A program may use at most 128 MiB of HBM per device.

```python
import jax
import jax.numpy as jnp
from jax import lax

L = 128
H = 128
LAYERS = 2
TILE = 256
DEG = 8
P_SIZE = 512
G = 128
E = 4096
GRID_X = 8
GRID_Y = 4


def draw_senders(key, part):
    key = jax.random.fold_in(key, 11)
    keys = jax.random.split(key, 4)
    layout_shape = (GRID_X, GRID_Y, E)
    choose = jax.random.randint(keys[0], layout_shape, 0, 10)
    local_rows = jax.random.randint(keys[1], layout_shape, 0, P_SIZE)
    direction = jax.random.randint(keys[2], layout_shape, 0, 8)
    direction = direction + (direction >= 4).astype(jnp.int32)
    position = jax.random.randint(keys[3], layout_shape, 0, G)
    result = jnp.where(choose < 3, P_SIZE + direction * G + position, local_rows)
    return result.at[0, 0, 0].set(P_SIZE + 9 * G - 1).astype(jnp.int32)


def draw_edge_count(key, part):
    key = jax.random.fold_in(key, 23)
    counts = E // 4 + jax.random.randint(key, (GRID_X, GRID_Y), 0, E - E // 4 + 1)
    return counts.at[0, 0].set(E).astype(jnp.int32)


def place_ends(values, key, least, top_value):
    longest = values.shape.index(max(values.shape))
    spots = []
    for shift in (0, 1):
        where = [jax.random.randint(jax.random.fold_in(key, axis), (), 0, length) for axis, length in enumerate(values.shape)]
        where[longest] = (where[longest] + shift) % values.shape[longest]
        spots.append(tuple(where))
    return values.at[spots[0]].set(least).at[spots[1]].set(top_value)


def levels(rng, extent, shards, low, high):
    def one(axis_at, shards_of):
        heights = jax.random.uniform(jax.random.fold_in(jax.random.fold_in(rng, 6), axis_at), (shards_of,), jnp.float32, low / len(shards), high / len(shards))
        return jnp.repeat(jnp.exp(heights), extent[axis_at] // shards_of).reshape((-1,) + (1,) * (len(extent) - axis_at - 1))

    level = one(*shards[0])
    for cut in shards[1:]:
        level = level * one(*cut)
    return level


def noise(own_key, dims, scale, bound, cuts=(), kind=jnp.bfloat16):
    gain = levels(own_key, dims, cuts, -0.22, 0.18) if cuts else 1.0
    array = jax.random.normal(own_key, dims, jnp.float32) * scale * gain
    return jnp.minimum(jnp.maximum(array, -bound), bound).astype(kind)


def setup_inputs(seed: int = 0) -> dict:
    streams_of = jax.random.split(jax.random.key(seed), 15)
    latents = noise(streams_of[0], (GRID_X, GRID_Y, P_SIZE, L), 1.0, 6.0, ((0, 8), (1, 4)))
    edge_latents = noise(streams_of[1], (GRID_X, GRID_Y, E, L), 1.0, 6.0, ((0, 8), (1, 4)))
    senders = draw_senders(jax.random.fold_in(streams_of[14], 71), 0)
    receivers = place_ends(jax.random.randint(streams_of[3], (GRID_X, GRID_Y, E), 0, TILE), jax.random.fold_in(streams_of[3], 1), 0, TILE - 1).astype(jnp.int32)
    ghost_rows = place_ends(jax.random.randint(streams_of[4], (GRID_X, GRID_Y, 3, 3, G), 0, P_SIZE), jax.random.fold_in(streams_of[4], 1), 0, P_SIZE - 1).astype(jnp.int32)
    edge_count = draw_edge_count(jax.random.fold_in(streams_of[14], 71), 0)
    node_cotangent = noise(streams_of[6], (GRID_X, GRID_Y, P_SIZE, L), 1.0, 6.0, ((0, 8), (1, 4)))
    edge_cotangent = noise(streams_of[7], (GRID_X, GRID_Y, E, L), 1.0, 6.0, ((0, 8), (1, 4)))
    edge_first = noise(streams_of[8], (LAYERS, 3 * L, H), (3 * L) ** -0.5, 0.3125)
    edge_second = noise(streams_of[9], (LAYERS, H, L), H ** -0.5, 0.5)
    edge_scale = jnp.clip(1.0 + 0.1 * jax.random.normal(streams_of[10], (LAYERS, L), jnp.float32), 0.5, 1.5)
    node_first = noise(streams_of[11], (LAYERS, 2 * L, H), (2 * L) ** -0.5, 0.375)
    node_second = noise(streams_of[12], (LAYERS, H, L), H ** -0.5, 0.5)
    node_scale = jnp.clip(1.0 + 0.1 * jax.random.normal(streams_of[13], (LAYERS, L), jnp.float32), 0.5, 1.5)
    return dict(latents=latents, edge_latents=edge_latents, senders=senders, receivers=receivers, ghost_rows=ghost_rows, edge_count=edge_count, node_cotangent=node_cotangent, edge_cotangent=edge_cotangent, edge_first=edge_first, edge_second=edge_second, edge_scale=edge_scale, node_first=node_first, node_second=node_second, node_scale=node_scale)


epsilon = 1e-05

def normalize(values, gains):
    center = lax.optimization_barrier(jnp.mean(values, axis=-1, keepdims=True))
    spread = lax.optimization_barrier(jnp.mean(jnp.square(values - center), axis=-1, keepdims=True))
    return (values - center) * lax.rsqrt(spread + epsilon) * gains

def layer_update(node32, ghost32, edge32, sender_ids, receiver_ids, edge_total, params):
    edge_first, edge_second, edge_scale, node_first, node_second, node_scale = params
    blocks = sender_ids.shape[0] // TILE
    node_table = jnp.concatenate([node32, ghost32.reshape(-1, L)], axis=0)
    sender_rows = jnp.take(node_table, sender_ids, axis=0).astype(jnp.bfloat16)
    onehot = (receiver_ids.reshape(blocks, TILE)[:, :, None] == jnp.arange(TILE, dtype=jnp.int32)[None, None, :]).astype(jnp.float32)
    tile_rows = jnp.repeat(node32.reshape(-1, TILE, L), DEG, axis=0)
    received = jnp.einsum('bei,bil->bel', onehot, tile_rows, precision=lax.Precision.HIGHEST).reshape(-1, L).astype(jnp.bfloat16)
    joined = jnp.concatenate([sender_rows, received, edge32.astype(jnp.bfloat16)], axis=1)
    edge_hidden = jax.nn.silu(jnp.dot(joined, edge_first.astype(jnp.bfloat16), preferred_element_type=jnp.float32)).astype(jnp.bfloat16)
    live_mask = (jnp.arange(sender_ids.shape[0], dtype=jnp.int32) < edge_total).astype(jnp.float32)[:, None]
    message = normalize(jnp.dot(edge_hidden, edge_second.astype(jnp.bfloat16), preferred_element_type=jnp.float32), edge_scale) * live_mask
    edge_next = (edge32 + message).astype(jnp.bfloat16)
    message_b = message.astype(jnp.bfloat16)
    summed = jnp.einsum('bei,bel->bil', onehot, message_b.astype(jnp.float32).reshape(blocks, TILE, L), precision=lax.Precision.HIGHEST)
    inbound = summed.reshape(-1, DEG, TILE, L).sum(axis=1).reshape(-1, L).astype(jnp.bfloat16)
    node_input = jnp.concatenate([node32.astype(jnp.bfloat16), inbound], axis=1)
    node_hidden = jax.nn.silu(jnp.dot(node_input, node_first.astype(jnp.bfloat16), preferred_element_type=jnp.float32)).astype(jnp.bfloat16)
    update = normalize(jnp.dot(node_hidden, node_second.astype(jnp.bfloat16), preferred_element_type=jnp.float32), node_scale)
    node_next = (node32 + update).astype(jnp.bfloat16)
    return (node_next, edge_next)

def gather_ghosts(node32, ghost_rows):
    picked = jax.vmap(jax.vmap(lambda source, indices: jnp.take(source, indices, axis=0)))(node32, ghost_rows)
    outside = jnp.ones((3, 3), jnp.float32).at[1, 1].set(0.0)
    picked = picked * outside[:, :, None, None]
    flipped = picked[:, :, ::-1, ::-1]
    padded = jnp.pad(flipped, ((1, 1), (1, 1), (0, 0), (0, 0), (0, 0), (0, 0)))
    slot_rows = []
    for row_slot in range(3):
        columns = [padded[row_slot:row_slot + GRID_X, col_slot:col_slot + GRID_Y, row_slot, col_slot] for col_slot in range(3)]
        slot_rows.append(jnp.stack(columns, axis=2))
    return jnp.stack(slot_rows, axis=2)

def flatten_domains(values):
    return values.reshape((GRID_X * GRID_Y,) + values.shape[2:])

def reference(latents, edge_latents, senders, receivers, ghost_rows, edge_count, node_cotangent, edge_cotangent, edge_first, edge_second, edge_scale, node_first, node_second, node_scale):
    params32 = (edge_first.astype(jnp.float32), edge_second.astype(jnp.float32), edge_scale.astype(jnp.float32), node_first.astype(jnp.float32), node_second.astype(jnp.float32), node_scale.astype(jnp.float32))

    def forward(node32, edge32, params):
        nodes_b = latents
        edges_b = edge_latents
        for layer_index in range(LAYERS):
            ghosts = gather_ghosts(node32, ghost_rows)
            layer_params = tuple((weights[layer_index] for weights in params))

            def domain(packed):
                return layer_update(packed[0], packed[1], packed[2], packed[3], packed[4], packed[5], layer_params)
            node_next, edge_next = lax.map(jax.checkpoint(domain), (flatten_domains(node32), flatten_domains(ghosts), flatten_domains(edge32), flatten_domains(senders), flatten_domains(receivers), flatten_domains(edge_count)))
            nodes_b = node_next.reshape(node32.shape)
            edges_b = edge_next.reshape(edge32.shape)
            node32 = nodes_b.astype(jnp.float32)
            edge32 = edges_b.astype(jnp.float32)
        return (nodes_b, edges_b)
    outputs, pullback = jax.vjp(forward, latents.astype(jnp.float32), edge_latents.astype(jnp.float32), params32)
    latents_grad, edge_latents_grad, grads = pullback((node_cotangent, edge_cotangent))
    return (outputs[0], outputs[1], latents_grad, edge_latents_grad, grads[0], grads[1], grads[2], grads[3], grads[4], grads[5])
```

```python
import functools

import jax
import jax.numpy as jnp
from jax import lax
from jax.experimental import pallas as pl
from jax.experimental.pallas import tpu as pltpu
from jax.sharding import PartitionSpec as P

L = 128
LAYERS = 2
TILE = 256
DEG = 8
SPAN = TILE * DEG
EPS = 1e-05
MESH = pl.DeviceIdType.MESH
F32 = jnp.float32
BF = jnp.bfloat16
VMEM = pl.BlockSpec(memory_space=pltpu.VMEM)
SMEM = pl.BlockSpec(memory_space=pltpu.SMEM)
OFFSETS = [(a - 1, b - 1) for a in range(3) for b in range(3) if (a, b) != (1, 1)]
SLOTS = len(OFFSETS)


def mm(a, b):
    return jnp.dot(a, b, preferred_element_type=F32)


def mm_nt(a, b):
    return lax.dot_general(a, b, (((1,), (1,)), ((), ())), preferred_element_type=F32)


def mm_tn(a, b):
    return lax.dot_general(a, b, (((0,), (0,)), ((), ())), preferred_element_type=F32)


def hot(mask):
    return jnp.where(mask, 1.0, 0.0).astype(BF)


def down(ids_row, width=L):
    n = ids_row.shape[1]
    return jnp.broadcast_to(ids_row, (L, n)).T


def picks(column, size):
    lane = lax.broadcasted_iota(jnp.int32, column.shape, 1)
    return jnp.concatenate([hot(column == lane + k) for k in range(0, size, L)], axis=1)


def drops(ids_row, first, size):
    row = lax.broadcasted_iota(jnp.int32, (size, ids_row.shape[1]), 0)
    return hot(row + first == ids_row)


def silu(v):
    return v / (1.0 + jnp.exp(-v))


def silu_slope(v):
    s = 1.0 / (1.0 + jnp.exp(-v))
    return s * (1.0 + v * (1.0 - s))


def standard(v):
    center = jnp.mean(v, axis=-1, keepdims=True)
    off = v - center
    inv = lax.rsqrt(jnp.mean(off * off, axis=-1, keepdims=True) + EPS)
    return off * inv, inv


def standard_back(g, hat, inv):
    a = jnp.mean(g, axis=-1, keepdims=True)
    b = jnp.mean(g * hat, axis=-1, keepdims=True)
    return inv * (g - a - hat * b)


def live(count, b):
    row = lax.broadcasted_iota(jnp.int32, (TILE, L), 0) + b * TILE
    return jnp.where(row < count, 1.0, 0.0)


def rows_of(b):
    return pl.ds(pl.multiple_of(b * TILE, TILE), TILE)


def forward(nodes, ghosts, edges, send, recv, count, w, table, msg, pre_out, edges_out,
            inb_out, nodes_out):
    ef, es, esc, nf, ns, nsc = w
    p = nodes.shape[0]
    size = p + ghosts.shape[0]
    blocks = edges.shape[0] // TILE
    ws, wr, we = (ef[i * L:(i + 1) * L, :] for i in range(3))
    table[:p, :] = mm(nodes[...], ws).astype(BF)
    table[p:size, :] = mm(ghosts[...], ws).astype(BF)
    table[size:size + p, :] = mm(nodes[...], wr).astype(BF)

    def block(b, carry):
        rows = rows_of(b)
        tile = pl.ds(pl.multiple_of(size + (b // DEG) * TILE, TILE), TILE)
        pre = (
            mm(picks(down(send[pl.ds(b, 1), :]), size), table[:size, :])
            + mm(picks(down(recv[pl.ds(b, 1), :]), TILE), table[tile, :])
            + mm(edges[rows, :], we)
        )
        pre_out[rows, :] = pre
        hat, _ = standard(mm(silu(pre).astype(BF), es[...]))
        message = hat * esc[...] * live(count, b)
        edges_out[rows, :] = (edges[rows, :].astype(F32) + message).astype(BF)
        msg[rows, :] = message.astype(BF)
        return carry

    lax.fori_loop(0, blocks, block, 0, unroll=2)
    for t in range(p // TILE):
        total = jnp.zeros((TILE, L), F32)
        for j in range(DEG):
            b = t * DEG + j
            total += mm(drops(recv[b:b + 1, :], 0, TILE), msg[b * TILE:(b + 1) * TILE, :])
        inb_out[t * TILE:(t + 1) * TILE, :] = total.astype(BF)
    pre_n = mm(nodes[...], nf[:L, :]) + mm(inb_out[...], nf[L:, :])
    hat, _ = standard(mm(silu(pre_n).astype(BF), ns[...]))
    nodes_out[...] = (nodes[...].astype(F32) + hat * nsc[...]).astype(BF)


def backward(nodes, ghosts, edges, send, send_flat, recv, count, w, pre_in, inb, node_ct, edge_ct,
             hid, du, dpre, edge_grad, ghost_grad, grads):
    ef, es, esc, nf, ns, nsc = w
    p = nodes.shape[0]
    ghost_n = ghosts.shape[0]
    blocks = edges.shape[0] // TILE
    ws, wr, we = (ef[i * L:(i + 1) * L, :] for i in range(3))
    nb = nodes[...]
    pre_n = mm(nb, nf[:L, :]) + mm(inb[...], nf[L:, :])
    hid_n = silu(pre_n).astype(BF)
    hat, inv = standard(mm(hid_n, ns[...]))
    node_scale_grad = jnp.sum(node_ct * hat, axis=0, keepdims=True)
    du_n = standard_back(node_ct * nsc[...], hat, inv).astype(BF)
    dpre_n = (mm_nt(du_n, ns[...]).astype(BF).astype(F32) * silu_slope(pre_n)).astype(BF)
    grads[512:640, :] = mm_tn(nb, dpre_n)
    grads[640:768, :] = mm_tn(inb[...], dpre_n)
    grads[768:896, :] = mm_tn(hid_n, du_n)
    node_grad = node_ct + mm_nt(dpre_n, nf[:L, :])
    dinb = mm_nt(dpre_n, nf[L:, :]).astype(BF)
    tiles = [dinb[t * TILE:(t + 1) * TILE, :] for t in range(p // TILE)]

    def block(tile_grad):
        def body(b, scale_grad):
            rows = rows_of(b)
            pre = pre_in[rows, :]
            h = silu(pre).astype(BF)
            hat, inv = standard(mm(h, es[...]))
            ect = edge_ct[rows, :].astype(F32)
            dm = (ect + mm(picks(down(recv[pl.ds(b, 1), :]), TILE), tile_grad)) * live(count, b)
            scale_grad = scale_grad + jnp.sum(dm * hat, axis=0, keepdims=True)
            d = standard_back(dm * esc[...], hat, inv).astype(BF)
            dp = (mm_nt(d, es[...]) * silu_slope(pre)).astype(BF)
            hid[rows, :] = h
            du[rows, :] = d
            dpre[rows, :] = dp
            edge_grad[rows, :] = (ect + mm_nt(dp, we)).astype(edge_grad.dtype)
            return scale_grad
        return body

    scale_grad = jnp.zeros((1, L), F32)
    for t, tile_grad in enumerate(tiles):
        scale_grad = lax.fori_loop(t * DEG, (t + 1) * DEG, block(tile_grad), scale_grad, unroll=2)
    grads[384:512, :] = mm_tn(hid[...], du[...])
    grads[256:384, :] = mm_tn(edges[...], dpre[...])
    row = lax.broadcasted_iota(jnp.int32, (16, L), 0)
    grads[896:912, :] = jnp.where(row == 0, scale_grad, jnp.where(row == 1, node_scale_grad, 0.0))
    parts = []
    for t in range(p // TILE):
        total = jnp.zeros((TILE, L), F32)
        for j in range(DEG):
            b = t * DEG + j
            total += mm(drops(recv[b:b + 1, :], 0, TILE), dpre[b * TILE:(b + 1) * TILE, :])
        parts.append(total.astype(BF))
    gr = jnp.concatenate(parts, axis=0)
    grads[L:2 * L, :] = mm_tn(nb, gr)
    node_grad = node_grad + mm_nt(gr, wr)
    ids = send_flat[...]
    parts = [
        mm(drops(ids, k, L), dpre[...]).astype(BF) for k in range(0, p + ghost_n, L)
    ]
    gs = jnp.concatenate(parts[:p // L], axis=0)
    gg = jnp.concatenate(parts[p // L:], axis=0)
    grads[:L, :] = mm_tn(nb, gs) + mm_tn(ghosts[...], gg)
    ghost_grad[...] = mm_nt(gg, ws).astype(BF)
    return node_grad + mm_nt(gs, ws)


def pick_ghosts(nodes, ghost_ids, picked):
    for c in range(SLOTS):
        picked[c * L:(c + 1) * L, :] = mm(
            picks(down(ghost_ids[c:c + 1, :]), nodes.shape[0]), nodes[...]
        ).astype(BF)


def put_back(ghost_flat, returned, p):
    return jnp.concatenate(
        [mm(drops(ghost_flat[...], k, L), returned[...]) for k in range(0, p, L)], axis=0
    )


def pick_kernel(nodes, ghost_ids, picked):
    pick_ghosts(nodes, ghost_ids, picked)


def first_kernel(count, nodes, ghosts, edges, send, recv, ghost_ids, ef, es, esc, nf, ns, nsc,
                 pre, edges_out, inb, nodes_out, picked, table, msg):
    forward(nodes, ghosts, edges, send, recv, count[0], (ef, es, esc, nf, ns, nsc), table, msg,
            pre, edges_out, inb, nodes_out)
    pick_ghosts(nodes_out, ghost_ids, picked)


def last_kernel(count, nodes, ghosts, edges, send, send_flat, recv, node_ct, edge_ct, ef, es, esc,
                nf, ns, nsc, edges_out, nodes_out, edge_grad, ghost_grad, grads, node_grad,
                table, msg, pre, inb, hid, du, dpre):
    w = (ef, es, esc, nf, ns, nsc)
    forward(nodes, ghosts, edges, send, recv, count[0], w, table, msg, pre, edges_out, inb,
            nodes_out)
    node_grad[...] = backward(nodes, ghosts, edges, send, send_flat, recv, count[0], w, pre, inb,
                              node_ct[...].astype(F32), edge_ct, hid, du, dpre, edge_grad,
                              ghost_grad, grads)


def low_kernel(count, nodes, ghosts, edges, send, send_flat, recv, ghost_flat, upper_grad,
               returned, edge_ct, pre, inb, ef, es, esc, nf, ns, nsc,
               edge_grad, ghost_grad, grads, node_grad, hid, du, dpre):
    w = (ef, es, esc, nf, ns, nsc)
    ct = upper_grad[...] + put_back(ghost_flat, returned, nodes.shape[0])
    node_grad[...] = backward(nodes, ghosts, edges, send, send_flat, recv, count[0], w, pre, inb,
                              ct.astype(BF).astype(F32), edge_ct, hid, du, dpre, edge_grad,
                              ghost_grad, grads)


def neighbours(gx, gy):
    x, y = lax.axis_index("gx"), lax.axis_index("gy")
    found = []
    for dx, dy in OFFSETS:
        there = (x + dx >= 0) & (x + dx < gx) & (y + dy >= 0) & (y + dy < gy)
        found.append((there, (lax.rem(x + dx + gx, gx), lax.rem(y + dy + gy, gy))))
    return found


def swap(found, src, dst, send_sem, recv_sem):
    copies = [
        pltpu.make_async_remote_copy(
            src_ref=src.at[c],
            dst_ref=dst.at[SLOTS - 1 - c],
            send_sem=send_sem.at[c],
            recv_sem=recv_sem.at[SLOTS - 1 - c],
            device_id=place,
            device_id_type=MESH,
        )
        for c, (_, place) in enumerate(found)
    ]
    for (there, _), copy in zip(found, copies):
        pl.when(there)(copy.start)
    return copies


def finish_swap(found, copies, src, dst, send_sem, recv_sem):
    for c, ((there, place), copy) in enumerate(zip(found, copies)):
        pl.when(there)(copy.wait_send)
        arrival = pltpu.make_async_remote_copy(
            src_ref=src.at[c], dst_ref=dst.at[c], send_sem=send_sem.at[c],
            recv_sem=recv_sem.at[c], device_id=place, device_id_type=MESH,
        )
        pl.when(there)(arrival.wait_recv)


def swap_kernel(gx, gy, src, dst, send_sem, recv_sem):
    found = neighbours(gx, gy)
    barrier = pltpu.get_barrier_semaphore()
    for there, place in found:
        @pl.when(there)
        def _():
            pl.semaphore_signal(barrier, inc=1, device_id=place, device_id_type=MESH)
    for c, (there, _) in enumerate(found):
        @pl.when(jnp.logical_not(there))
        def _():
            dst[c] = jnp.zeros(dst.shape[1:], dst.dtype)
    peers = sum(jnp.where(there, 1, 0) for there, _ in found)
    pl.semaphore_wait(barrier, peers)
    copies = swap(found, src, dst, send_sem, recv_sem)
    finish_swap(found, copies, src, dst, send_sem, recv_sem)


def solution(mesh):
    gx, gy = mesh.shape["gx"], mesh.shape["gy"]

    def call(kernel, shapes, scratch, args, smem_first=True, **params):
        return pl.pallas_call(
            kernel,
            out_shape=shapes,
            in_specs=[SMEM if smem_first and i == 0 else VMEM for i in range(len(args))],
            out_specs=jax.tree.map(lambda _: VMEM, shapes),
            scratch_shapes=scratch,
            compiler_params=pltpu.CompilerParams(vmem_limit_bytes=48 * 2**20, **params),
        )(*args)

    def exchange(value, collective_id):
        shape = (SLOTS, value.shape[0] // SLOTS, L)
        out = call(
            functools.partial(swap_kernel, gx, gy),
            jax.ShapeDtypeStruct(shape, BF),
            [pltpu.SemaphoreType.DMA((SLOTS,)), pltpu.SemaphoreType.DMA((SLOTS,))],
            (value.reshape(shape),),
            smem_first=False,
            collective_id=collective_id,
            has_side_effects=True,
        )
        return out.reshape(value.shape)

    def on_device(latents, edge_latents, senders, receivers, ghost_rows, edge_count,
                  node_cotangent, edge_cotangent, edge_first, edge_second, edge_scale,
                  node_first, node_second, node_scale):
        nodes, edges = latents[0, 0], edge_latents[0, 0]
        p, e = nodes.shape[0], edges.shape[0]
        g = ghost_rows.shape[-1]
        ghost_n = SLOTS * g
        ids = senders[0, 0]
        ids = jnp.where(ids >= p + 4 * g, ids - g, ids)
        send, send_flat = ids.reshape(-1, TILE), ids.reshape(1, -1)
        recv = receivers[0, 0].reshape(-1, TILE)
        slots = ghost_rows[0, 0].reshape(9, g)
        ghost_ids = jnp.concatenate([slots[:4], slots[5:]], axis=0)
        ghost_flat = ghost_ids.reshape(1, -1)
        count = edge_count.reshape(1)
        weights = [
            (edge_first[i], edge_second[i], edge_scale[i:i + 1], node_first[i], node_second[i],
             node_scale[i:i + 1])
            for i in range(LAYERS)
        ]

        def s(shape, dtype):
            return jax.ShapeDtypeStruct(shape, dtype)

        back_scratch = [pltpu.VMEM((e, L), BF)] * 3
        fore_scratch = [pltpu.VMEM((2 * p + ghost_n, L), BF), pltpu.VMEM((e, L), BF)]
        grad_rows = s((912, L), F32)

        picked = call(pick_kernel, s((ghost_n, L), BF), [], (nodes, ghost_ids), smem_first=False)
        ghosts0 = exchange(picked, 0)
        pre0, edges1, inb0, nodes1, picked1 = call(
            first_kernel,
            (s((e, L), F32), s((e, L), BF), s((p, L), BF), s((p, L), BF), s((ghost_n, L), BF)),
            fore_scratch,
            (count, nodes, ghosts0, edges, send, recv, ghost_ids, *weights[0]),
        )
        ghosts1 = exchange(picked1, 1)
        edges_out, nodes_out, edge_ct, ghost_ct, grads1, upper = call(
            last_kernel,
            (s((e, L), BF), s((p, L), BF), s((e, L), BF), s((ghost_n, L), BF), grad_rows,
             s((p, L), F32)),
            fore_scratch + [pltpu.VMEM((e, L), F32), pltpu.VMEM((p, L), BF)] + back_scratch,
            (count, nodes1, ghosts1, edges1, send, send_flat, recv, node_cotangent[0, 0],
             edge_cotangent[0, 0], *weights[1]),
        )
        total1 = lax.psum(grads1, ("gx", "gy"))
        returned1 = exchange(ghost_ct, 2)
        edge_grad, ghost_ct0, grads0, lower = call(
            low_kernel,
            (s((e, L), F32), s((ghost_n, L), BF), grad_rows, s((p, L), F32)),
            back_scratch,
            (count, nodes, ghosts0, edges, send, send_flat, recv, ghost_flat, upper, returned1,
             edge_ct, pre0, inb0, *weights[0]),
        )
        total0 = lax.psum(grads0, ("gx", "gy"))
        returned0 = exchange(ghost_ct0, 3)

        def end_kernel(ids_ref, lower_ref, returned_ref, out):
            out[...] = lower_ref[...] + put_back(ids_ref, returned_ref, p)

        node_grad = call(end_kernel, s((p, L), F32), [], (ghost_flat, lower, returned0),
                         smem_first=False)
        totals = jnp.stack([total0, total1])
        return (
            nodes_out[None, None],
            edges_out[None, None],
            node_grad[None, None],
            edge_grad[None, None],
            totals[:, :384],
            totals[:, 384:512],
            totals[:, 896],
            totals[:, 512:768],
            totals[:, 768:896],
            totals[:, 897],
        )

    cell = P("gx", "gy", None, None)
    line = P("gx", "gy", None)
    return jax.shard_map(
        on_device,
        mesh=mesh,
        in_specs=(cell, cell, line, line, P("gx", "gy", None, None, None), P("gx", "gy"), cell,
                  cell) + (P(),) * 6,
        out_specs=(cell,) * 4 + (P(),) * 6,
        check_vma=False,
    )
```

```python
import functools

import jax
import jax.numpy as jnp
from jax import lax
from jax.experimental import pallas as pl
from jax.experimental.pallas import tpu as pltpu
from jax.sharding import PartitionSpec as P

L = 128
LAYERS = 2
TILE = 256
DEG = 8
SPAN = TILE * DEG
EPS = 1e-05
MESH = pl.DeviceIdType.MESH
F32 = jnp.float32
BF = jnp.bfloat16
I16 = jnp.int16
VMEM = pl.BlockSpec(memory_space=pltpu.VMEM)
SMEM = pl.BlockSpec(memory_space=pltpu.SMEM)
OFFSETS = [(a - 1, b - 1) for a in range(3) for b in range(3) if (a, b) != (1, 1)]
SLOTS = len(OFFSETS)


def mm(a, b):
    return jnp.dot(a, b, preferred_element_type=F32)


def mm_nt(a, b):
    return lax.dot_general(a, b, (((1,), (1,)), ((), ())), preferred_element_type=F32)


def mm_tn(a, b):
    return lax.dot_general(a, b, (((0,), (0,)), ((), ())), preferred_element_type=F32)


def hot(mask):
    return jnp.where(mask, jnp.ones((), BF), jnp.zeros((), BF))


def down(ids_row, width=L):
    n = ids_row.shape[1]
    return jnp.broadcast_to(ids_row, (L, n)).T.astype(I16)


def picks(column, size):
    lane = lax.broadcasted_iota(jnp.int32, column.shape, 1).astype(I16)
    return jnp.concatenate([hot(column == lane + jnp.int16(k)) for k in range(0, size, L)], axis=1)


def drops(ids_row, first, size):
    shape = (size, ids_row.shape[1])
    row = lax.broadcasted_iota(jnp.int32, shape, 0) + first
    return hot(row.astype(I16) == jnp.broadcast_to(ids_row, shape).astype(I16))


def silu(v):
    return v / (1.0 + jnp.exp(-v))


def silu_slope(v):
    s = 1.0 / (1.0 + jnp.exp(-v))
    return s * (1.0 + v * (1.0 - s))


def standard(v):
    center = jnp.mean(v, axis=-1, keepdims=True)
    off = v - center
    inv = lax.rsqrt(jnp.mean(off * off, axis=-1, keepdims=True) + EPS)
    return off * inv, inv


def standard_back(g, hat, inv):
    a = jnp.mean(g, axis=-1, keepdims=True)
    b = jnp.mean(g * hat, axis=-1, keepdims=True)
    return inv * (g - a - hat * b)


def live(count, b):
    row = lax.broadcasted_iota(jnp.int32, (TILE, L), 0) + b * TILE
    return jnp.where(row < count, 1.0, 0.0)


def rows_of(b):
    return pl.ds(pl.multiple_of(b * TILE, TILE), TILE)


def table_ids(ids, p, g):
    return jnp.where(ids >= p + 4 * g, ids - g, ids)


def ghost_row(ghost_ids, c):
    a, b = divmod(c + (c >= 4), 3)
    return ghost_ids[0, 0, a, b:b + 1, :]


def forward(nodes, ghosts, edges, send, recv, count, w, table, msg, pre_out, edges_out,
            inb_out, nodes_out):
    ef, es, esc, nf, ns, nsc = w
    p = nodes.shape[0]
    g = ghosts.shape[0] // SLOTS
    size = p + ghosts.shape[0]
    ws, wr, we = (ef[i * L:(i + 1) * L, :] for i in range(3))
    table[:p, :] = mm(nodes[...], ws).astype(BF)
    table[p:size, :] = mm(ghosts[...], ws).astype(BF)
    table[size + TILE:size + TILE + L, :] = we

    def block(b, carry):
        rows = rows_of(b)
        left = jnp.concatenate(
            [
                picks(down(table_ids(send[:, rows], p, g)), size),
                picks(down(recv[:, rows]), TILE),
                edges[rows, :],
            ],
            axis=1,
        )
        pre = mm(left, table[...])
        pre_out[rows, :] = pre
        hat, _ = standard(mm(silu(pre).astype(BF), es[...]))
        message = hat * esc[...] * live(count, b)
        edges_out[rows, :] = (edges[rows, :].astype(F32) + message).astype(BF)
        msg[rows, :] = message.astype(BF)
        return carry

    for t in range(p // TILE):
        table[size:size + TILE, :] = mm(nodes[t * TILE:(t + 1) * TILE, :], wr).astype(BF)
        lax.fori_loop(t * DEG, (t + 1) * DEG, block, 0, unroll=4)
    for t in range(p // TILE):
        total = jnp.zeros((TILE, L), F32)
        for j in range(DEG):
            b = t * DEG + j
            at = slice(b * TILE, (b + 1) * TILE)
            total += mm(drops(recv[:, at], 0, TILE), msg[at, :])
        inb_out[t * TILE:(t + 1) * TILE, :] = total.astype(BF)
    pre_n = mm(nodes[...], nf[:L, :]) + mm(inb_out[...], nf[L:, :])
    hat, _ = standard(mm(silu(pre_n).astype(BF), ns[...]))
    nodes_out[...] = (nodes[...].astype(F32) + hat * nsc[...]).astype(BF)


def backward(nodes, ghosts, edges, send, recv, count, w, pre_in, inb, node_ct, edge_ct,
             hid, du, dpre, edge_grad, ghost_grad, grads):
    ef, es, esc, nf, ns, nsc = w
    p = nodes.shape[0]
    ghost_n = ghosts.shape[0]
    blocks = edges.shape[0] // TILE
    ws, wr, we = (ef[i * L:(i + 1) * L, :] for i in range(3))
    nb = nodes[...]
    pre_n = mm(nb, nf[:L, :]) + mm(inb[...], nf[L:, :])
    hid_n = silu(pre_n).astype(BF)
    hat, inv = standard(mm(hid_n, ns[...]))
    node_scale_grad = jnp.sum(node_ct * hat, axis=0, keepdims=True)
    du_n = standard_back(node_ct * nsc[...], hat, inv).astype(BF)
    dpre_n = (mm_nt(du_n, ns[...]).astype(BF).astype(F32) * silu_slope(pre_n)).astype(BF)
    grads[512:640, :] = mm_tn(nb, dpre_n).astype(BF)
    grads[640:768, :] = mm_tn(inb[...], dpre_n).astype(BF)
    grads[768:896, :] = mm_tn(hid_n, du_n).astype(BF)
    node_grad = node_ct + mm_nt(dpre_n, nf[:L, :])
    dinb = mm_nt(dpre_n, nf[L:, :]).astype(BF)
    tiles = [dinb[t * TILE:(t + 1) * TILE, :] for t in range(p // TILE)]

    def block(tile_grad):
        def body(b, scale_grad):
            rows = rows_of(b)
            pre = pre_in[rows, :]
            h = silu(pre).astype(BF)
            hat, inv = standard(mm(h, es[...]))
            ect = edge_ct[rows, :].astype(F32)
            dm = (ect + mm(picks(down(recv[:, rows]), TILE), tile_grad)) * live(count, b)
            scale_grad = scale_grad + jnp.sum(dm * hat, axis=0, keepdims=True)
            d = standard_back(dm * esc[...], hat, inv).astype(BF)
            dp = (mm_nt(d, es[...]) * silu_slope(pre)).astype(BF)
            hid[rows, :] = h
            du[rows, :] = d
            dpre[rows, :] = dp
            edge_grad[rows, :] = (ect + mm_nt(dp, we)).astype(edge_grad.dtype)
            return scale_grad
        return body

    scale_grad = jnp.zeros((1, L), F32)
    for t, tile_grad in enumerate(tiles):
        scale_grad = lax.fori_loop(t * DEG, (t + 1) * DEG, block(tile_grad), scale_grad, unroll=4)
    grads[384:512, :] = mm_tn(hid[...], du[...]).astype(BF)
    grads[256:384, :] = mm_tn(edges[...], dpre[...]).astype(BF)
    row = lax.broadcasted_iota(jnp.int32, (16, L), 0)
    scales = jnp.where(row == 0, scale_grad, jnp.where(row == 1, node_scale_grad, 0.0))
    grads[896:912, :] = scales.astype(BF)
    parts = []
    for t in range(p // TILE):
        total = jnp.zeros((TILE, L), F32)
        for j in range(DEG):
            b = t * DEG + j
            at = slice(b * TILE, (b + 1) * TILE)
            total += mm(drops(recv[:, at], 0, TILE), dpre[at, :])
        parts.append(total.astype(BF))
    gr = jnp.concatenate(parts, axis=0)
    grads[L:2 * L, :] = mm_tn(nb, gr).astype(BF)
    node_grad = node_grad + mm_nt(gr, wr)
    ids = table_ids(send[...], p, ghost_n // SLOTS)
    parts = [
        mm(drops(ids, k, L), dpre[...]).astype(BF) for k in range(0, p + ghost_n, L)
    ]
    gs = jnp.concatenate(parts[:p // L], axis=0)
    gg = jnp.concatenate(parts[p // L:], axis=0)
    grads[:L, :] = (mm_tn(nb, gs) + mm_tn(ghosts[...], gg)).astype(BF)
    ghost_grad[...] = mm_nt(gg, ws).astype(BF)
    return node_grad + mm_nt(gs, ws)


def pick_ghosts(nodes, ghost_ids, picked):
    for c in range(SLOTS):
        picked[c * L:(c + 1) * L, :] = mm(
            picks(down(ghost_row(ghost_ids, c)), nodes.shape[0]), nodes[...]
        ).astype(BF)


def put_back(ghost_ids, returned, p):
    ids = jnp.concatenate([ghost_row(ghost_ids, c) for c in range(SLOTS)], axis=1)
    return jnp.concatenate([mm(drops(ids, k, L), returned[...]) for k in range(0, p, L)], axis=0)


def layer_of(i, ef, es, esc, nf, ns, nsc):
    return ef.at[i], es.at[i], esc.at[i:i + 1], nf.at[i], ns.at[i], nsc.at[i:i + 1]


def pick_kernel(nodes, ghost_ids, picked):
    pick_ghosts(nodes, ghost_ids, picked)


def first_kernel(count, nodes, ghosts, edges, send, recv, ghost_ids, ef, es, esc, nf, ns, nsc,
                 pre, edges_out, inb, nodes_out, picked, table, msg):
    forward(nodes, ghosts, edges, send, recv, count[0], layer_of(0, ef, es, esc, nf, ns, nsc), table, msg,
            pre, edges_out, inb, nodes_out)
    pick_ghosts(nodes_out, ghost_ids, picked)


def last_kernel(count, nodes, ghosts, edges, send, recv, node_ct, edge_ct, ef, es, esc,
                nf, ns, nsc, edges_out, nodes_out, edge_grad, ghost_grad, grads, node_grad,
                table, msg, pre, inb, hid, du, dpre):
    w = layer_of(1, ef, es, esc, nf, ns, nsc)
    forward(nodes, ghosts, edges, send, recv, count[0], w, table, msg, pre, edges_out, inb,
            nodes_out)
    node_grad[...] = backward(nodes, ghosts, edges, send, recv, count[0], w, pre, inb,
                              node_ct[...].astype(F32), edge_ct, hid, du, dpre, edge_grad,
                              ghost_grad, grads)


def low_kernel(count, nodes, ghosts, edges, send, recv, ghost_ids, upper_grad,
               returned, edge_ct, pre, inb, ef, es, esc, nf, ns, nsc,
               edge_grad, ghost_grad, grads, node_grad, hid, du, dpre):
    w = layer_of(0, ef, es, esc, nf, ns, nsc)
    ct = upper_grad[...] + put_back(ghost_ids, returned, nodes.shape[0])
    node_grad[...] = backward(nodes, ghosts, edges, send, recv, count[0], w, pre, inb,
                              ct.astype(BF).astype(F32), edge_ct, hid, du, dpre, edge_grad,
                              ghost_grad, grads)


def neighbours(gx, gy):
    x, y = lax.axis_index("gx"), lax.axis_index("gy")
    found = []
    for dx, dy in OFFSETS:
        there = (x + dx >= 0) & (x + dx < gx) & (y + dy >= 0) & (y + dy < gy)
        found.append((there, (lax.rem(x + dx + gx, gx), lax.rem(y + dy + gy, gy))))
    return found


def swap(found, src, dst, send_sem, recv_sem):
    copies = [
        pltpu.make_async_remote_copy(
            src_ref=src.at[c],
            dst_ref=dst.at[SLOTS - 1 - c],
            send_sem=send_sem.at[c],
            recv_sem=recv_sem.at[SLOTS - 1 - c],
            device_id=place,
            device_id_type=MESH,
        )
        for c, (_, place) in enumerate(found)
    ]
    for (there, _), copy in zip(found, copies):
        pl.when(there)(copy.start)
    return copies


def finish_swap(found, copies, src, dst, send_sem, recv_sem):
    for c, ((there, place), copy) in enumerate(zip(found, copies)):
        pl.when(there)(copy.wait_send)
        arrival = pltpu.make_async_remote_copy(
            src_ref=src.at[c], dst_ref=dst.at[c], send_sem=send_sem.at[c],
            recv_sem=recv_sem.at[c], device_id=place, device_id_type=MESH,
        )
        pl.when(there)(arrival.wait_recv)


def swap_kernel(gx, gy, src, dst, send_sem, recv_sem):
    found = neighbours(gx, gy)
    barrier = pltpu.get_barrier_semaphore()
    for there, place in found:
        @pl.when(there)
        def _():
            pl.semaphore_signal(barrier, inc=1, device_id=place, device_id_type=MESH)
    for c, (there, _) in enumerate(found):
        @pl.when(jnp.logical_not(there))
        def _():
            dst[c] = jnp.zeros(dst.shape[1:], dst.dtype)
    peers = sum(jnp.where(there, 1, 0) for there, _ in found)
    pl.semaphore_wait(barrier, peers)
    copies = swap(found, src, dst, send_sem, recv_sem)
    finish_swap(found, copies, src, dst, send_sem, recv_sem)


def reduce_kernel(gx, gy, rows, src, grads0, grads1, dst, total, packed, half, part, got_core,
                  got_x, got_gx, send_sem, recv_sem):
    x, y = lax.axis_index("gx"), lax.axis_index("gy")
    core, chip = lax.rem(y, 2), y // 2
    chips = gy // 2
    found = neighbours(gx, gy)
    keep = [rows // 2, rows // (2 * chips), rows // (2 * chips * gx)]
    start = [0, core * keep[0], core * keep[0] + chip * keep[1]]
    groups = [
        (2, core, lambda j: (x, chip * 2 + j)),
        (chips, chip, lambda j: (x, j * 2 + core)),
        (gx, x, lambda j: (j, y)),
    ]
    barrier = pltpu.get_barrier_semaphore()
    for there, place in found:
        @pl.when(there)
        def _():
            pl.semaphore_signal(barrier, inc=1, device_id=place, device_id_type=MESH)
    peers = sum(jnp.where(there, 1, 0) for there, _ in found)
    for count, me, place in groups:
        for d in range(1, count):
            pl.semaphore_signal(barrier, inc=1, device_id=place(lax.rem(me + d, count)),
                                device_id_type=MESH)
            peers = peers + 1
    for c, (there, _) in enumerate(found):
        @pl.when(jnp.logical_not(there))
        def _():
            dst[c] = jnp.zeros(dst.shape[1:], dst.dtype)
    n = grads0.shape[0]
    packed[:n, :] = grads0[...]
    packed[n:2 * n, :] = grads1[...]
    packed[2 * n:, :] = jnp.zeros((rows - 2 * n, L), BF)
    pl.semaphore_wait(barrier, peers)
    swaps = swap(found, src, dst, send_sem, recv_sem)

    def at(index, size):
        return pl.ds(pl.multiple_of(index, 16), size)

    sent = []
    sem = SLOTS
    held = packed
    for (count, me, place), size, got, out in zip(
        groups, keep, (got_core, got_x, got_gx), (half, part, total)
    ):
        copies = []
        for d in range(1, count):
            peer = lax.rem(me + d, count)
            copies.append(pltpu.make_async_remote_copy(
                src_ref=held.at[at(peer * size, size)], dst_ref=got.at[d - 1],
                send_sem=send_sem.at[sem], recv_sem=recv_sem.at[sem],
                device_id=place(peer), device_id_type=MESH,
            ))
            sem += 1
            copies[-1].start()
        mine = held[at(me * size, size), :].astype(F32)
        for d, copy in enumerate(copies):
            copy.wait_recv()
            mine = mine + got[d].astype(F32)
        if out is total:
            out[at(start[2] + x * size, size), :] = mine.astype(BF)
        else:
            out[...] = mine.astype(BF)
        sent += copies
        held = out
    for (count, me, place), size, first in reversed(list(zip(groups, keep, start))):
        copies = []
        own = total.at[at(first + me * size, size)]
        for d in range(1, count):
            copies.append(pltpu.make_async_remote_copy(
                src_ref=own, dst_ref=own, send_sem=send_sem.at[sem], recv_sem=recv_sem.at[sem],
                device_id=place(lax.rem(me + d, count)), device_id_type=MESH,
            ))
            copies[-1].start()
            origin = lax.rem(me - d + count, count)
            block = total.at[at(first + origin * size, size)]
            copies.append(pltpu.make_async_remote_copy(
                src_ref=block, dst_ref=block, send_sem=send_sem.at[sem], recv_sem=recv_sem.at[sem],
                device_id=place(origin), device_id_type=MESH,
            ))
            sem += 1
        for copy in copies[1::2]:
            copy.wait_recv()
        sent += copies[::2]
    for copy in sent:
        copy.wait_send()
    finish_swap(found, swaps, src, dst, send_sem, recv_sem)


def end_kernel(ghost_ids, lower, returned, total, node_grad, ef, es, esc, nf, ns, nsc):
    p = lower.shape[0]
    node_grad[...] = lower[...] + put_back(ghost_ids, returned, p)
    for i in range(LAYERS):
        base = i * 912
        for out, first, last in ((ef, 0, 384), (es, 384, 512), (nf, 512, 768), (ns, 768, 896)):
            out[i] = total[base + first:base + last, :].astype(F32)
        scales = total[base + 896:base + 912, :].astype(F32)
        esc[i:i + 1, :] = scales[:1, :]
        nsc[i:i + 1, :] = scales[1:2, :]


def solution(mesh):
    gx, gy = mesh.shape["gx"], mesh.shape["gy"]

    def call(kernel, shapes, scratch, args, smem_first=True, **params):
        return pl.pallas_call(
            kernel,
            out_shape=shapes,
            in_specs=[SMEM if smem_first and i == 0 else VMEM for i in range(len(args))],
            out_specs=jax.tree.map(lambda _: VMEM, shapes),
            scratch_shapes=scratch,
            compiler_params=pltpu.CompilerParams(vmem_limit_bytes=48 * 2**20, **params),
        )(*args)

    def exchange(value, collective_id):
        shape = (SLOTS, value.shape[0] // SLOTS, L)
        out = call(
            functools.partial(swap_kernel, gx, gy),
            jax.ShapeDtypeStruct(shape, BF),
            [pltpu.SemaphoreType.DMA((SLOTS,)), pltpu.SemaphoreType.DMA((SLOTS,))],
            (value.reshape(shape),),
            smem_first=False,
            collective_id=collective_id,
            has_side_effects=True,
        )
        return out.reshape(value.shape)

    def on_device(latents, edge_latents, senders, receivers, ghost_rows, edge_count,
                  node_cotangent, edge_cotangent, edge_first, edge_second, edge_scale,
                  node_first, node_second, node_scale):
        nodes, edges = latents[0, 0], edge_latents[0, 0]
        p, e = nodes.shape[0], edges.shape[0]
        ghost_n = SLOTS * ghost_rows.shape[-1]
        send, recv = senders.reshape(1, e), receivers.reshape(1, e)
        count = edge_count.reshape(1)
        weights = (edge_first, edge_second, edge_scale, node_first, node_second, node_scale)

        def s(shape, dtype):
            return jax.ShapeDtypeStruct(shape, dtype)

        back_scratch = [pltpu.VMEM((e, L), BF)] * 3
        fore_scratch = [pltpu.VMEM((p + ghost_n + TILE + L, L), BF), pltpu.VMEM((e, L), BF)]
        n = 912
        grad_rows = s((n, L), BF)

        picked = call(pick_kernel, s((ghost_n, L), BF), [], (nodes, ghost_rows), smem_first=False)
        ghosts0 = exchange(picked, 0)
        pre0, edges1, inb0, nodes1, picked1 = call(
            first_kernel,
            (s((e, L), F32), s((e, L), BF), s((p, L), BF), s((p, L), BF), s((ghost_n, L), BF)),
            fore_scratch,
            (count, nodes, ghosts0, edges, send, recv, ghost_rows, *weights),
        )
        ghosts1 = exchange(picked1, 1)
        edges_out, nodes_out, edge_ct, ghost_ct, grads1, upper = call(
            last_kernel,
            (s((e, L), BF), s((p, L), BF), s((e, L), BF), s((ghost_n, L), BF), grad_rows,
             s((p, L), F32)),
            fore_scratch + [pltpu.VMEM((e, L), F32), pltpu.VMEM((p, L), BF)] + back_scratch,
            (count, nodes1, ghosts1, edges1, send, recv, node_cotangent[0, 0],
             edge_cotangent[0, 0], *weights),
        )
        returned1 = exchange(ghost_ct, 2)
        edge_grad, ghost_ct0, grads0, lower = call(
            low_kernel,
            (s((e, L), F32), s((ghost_n, L), BF), grad_rows, s((p, L), F32)),
            back_scratch,
            (count, nodes, ghosts0, edges, send, recv, ghost_rows, upper, returned1,
             edge_ct, pre0, inb0, *weights),
        )
        unit = 16 * gx * gy
        rows = -(-2 * n // unit) * unit
        chips = gy // 2
        quarter = rows // (2 * chips)
        sems = SLOTS + 2 * (1 + chips - 1 + gx - 1)
        slots = (SLOTS, ghost_n // SLOTS, L)
        returned0, total = call(
            functools.partial(reduce_kernel, gx, gy, rows),
            (s(slots, BF), s((rows, L), BF)),
            [pltpu.VMEM((rows, L), BF), pltpu.VMEM((rows // 2, L), BF), pltpu.VMEM((quarter, L), BF),
             pltpu.VMEM((1, rows // 2, L), BF), pltpu.VMEM((chips - 1, quarter, L), BF),
             pltpu.VMEM((gx - 1, quarter // gx, L), BF),
             pltpu.SemaphoreType.DMA((sems,)), pltpu.SemaphoreType.DMA((sems,))],
            (ghost_ct0.reshape(slots), grads0, grads1),
            smem_first=False,
            collective_id=3,
            has_side_effects=True,
        )
        node_grad, *weight_grads = call(
            end_kernel,
            (s((p, L), F32),) + tuple(s(w.shape, F32) for w in weights),
            [],
            (ghost_rows, lower, returned0.reshape(ghost_n, L), total),
            smem_first=False,
        )
        return (
            nodes_out[None, None],
            edges_out[None, None],
            node_grad[None, None],
            edge_grad[None, None],
            *weight_grads,
        )

    cell = P("gx", "gy", None, None)
    line = P("gx", "gy", None)
    return jax.shard_map(
        on_device,
        mesh=mesh,
        in_specs=(cell, cell, line, line, P("gx", "gy", None, None, None), P("gx", "gy"), cell,
                  cell) + (P(),) * 6,
        out_specs=(cell,) * 4 + (P(),) * 6,
        check_vma=False,
    )
```

```python
import functools

import jax
import jax.numpy as jnp
from jax import lax
from jax.experimental import pallas as pl
from jax.experimental.pallas import tpu as pltpu
from jax.sharding import PartitionSpec as P

L = 128
LAYERS = 2
TILE = 256
DEG = 8
SPAN = TILE * DEG
EPS = 1e-05
MESH = pl.DeviceIdType.MESH
F32 = jnp.float32
BF = jnp.bfloat16
I16 = jnp.int16
VMEM = pl.BlockSpec(memory_space=pltpu.VMEM)
SMEM = pl.BlockSpec(memory_space=pltpu.SMEM)
OFFSETS = [(a - 1, b - 1) for a in range(3) for b in range(3) if (a, b) != (1, 1)]
SLOTS = len(OFFSETS)


def mm(a, b):
    return jnp.dot(a, b, preferred_element_type=F32)


def mm_nt(a, b):
    return lax.dot_general(a, b, (((1,), (1,)), ((), ())), preferred_element_type=F32)


def mm_tn(a, b):
    return lax.dot_general(a, b, (((0,), (0,)), ((), ())), preferred_element_type=F32)


def hot(mask):
    return jnp.where(mask, jnp.ones((), BF), jnp.zeros((), BF))


def down(ids_row, width=L):
    n = ids_row.shape[1]
    return jnp.broadcast_to(ids_row, (L, n)).T.astype(I16)


def picks(column, size):
    lane = lax.broadcasted_iota(jnp.int32, column.shape, 1).astype(I16)
    return jnp.concatenate([hot(column == lane + jnp.int16(k)) for k in range(0, size, L)], axis=1)


def drops(ids_row, first, size):
    shape = (size, ids_row.shape[1])
    row = lax.broadcasted_iota(jnp.int32, shape, 0) + first
    return hot(row.astype(I16) == jnp.broadcast_to(ids_row, shape).astype(I16))


def silu(v):
    return v / (1.0 + jnp.exp(-v))


def silu_parts(v):
    s = 1.0 / (1.0 + jnp.exp(-v))
    return v * s, s * (1.0 + v * (1.0 - s))


def standard(v):
    center = jnp.mean(v, axis=-1, keepdims=True)
    off = v - center
    inv = lax.rsqrt(jnp.mean(off * off, axis=-1, keepdims=True) + EPS)
    return off * inv, inv


def standard_back(g, hat, inv):
    a = jnp.mean(g, axis=-1, keepdims=True)
    b = jnp.mean(g * hat, axis=-1, keepdims=True)
    return inv * (g - a - hat * b)


def live(count, b):
    row = lax.broadcasted_iota(jnp.int32, (TILE, L), 0) + b * TILE
    return jnp.where(row < count, 1.0, 0.0)


def rows_of(b):
    return pl.ds(pl.multiple_of(b * TILE, TILE), TILE)


def table_ids(ids, p, g):
    return jnp.where(ids >= p + 4 * g, ids - g, ids)


def ghost_row(ghost_ids, c):
    a, b = divmod(c + (c >= 4), 3)
    return ghost_ids[0, 0, a, b:b + 1, :]


def forward(nodes, ghosts, edges, send_down, recv, recv_down, count, w, table, msg, pre_out, edges_out,
            inb_out, nodes_out):
    ef, es, esc, nf, ns, nsc = w
    p = nodes.shape[0]
    size = p + ghosts.shape[0]
    ws, wr, we = (ef[i * L:(i + 1) * L, :] for i in range(3))
    table[:p, :] = mm(nodes[...], ws).astype(BF)
    table[p:size, :] = mm(ghosts[...], ws).astype(BF)
    table[size + TILE:size + TILE + L, :] = we

    def block(b, carry):
        rows = rows_of(b)
        left = jnp.concatenate(
            [
                picks(send_down[rows, :], size),
                picks(recv_down[rows, :], TILE),
                edges[rows, :],
            ],
            axis=1,
        )
        pre = mm(left, table[...])
        pre_out[rows, :] = pre
        hat, _ = standard(mm(silu(pre).astype(BF), es[...]))
        message = hat * esc[...] * live(count, b)
        edges_out[rows, :] = (edges[rows, :].astype(F32) + message).astype(BF)
        msg[rows, :] = message.astype(BF)
        return carry

    for t in range(p // TILE):
        table[size:size + TILE, :] = mm(nodes[t * TILE:(t + 1) * TILE, :], wr).astype(BF)
        lax.fori_loop(t * DEG, (t + 1) * DEG, block, 0, unroll=4)
    for t in range(p // TILE):
        total = jnp.zeros((TILE, L), F32)
        for j in range(DEG):
            b = t * DEG + j
            at = slice(b * TILE, (b + 1) * TILE)
            total += mm(drops(recv[:, at], 0, TILE), msg[at, :])
        inb_out[t * TILE:(t + 1) * TILE, :] = total.astype(BF)
    pre_n = mm(nodes[...], nf[:L, :]) + mm(inb_out[...], nf[L:, :])
    hat, _ = standard(mm(silu(pre_n).astype(BF), ns[...]))
    nodes_out[...] = (nodes[...].astype(F32) + hat * nsc[...]).astype(BF)


def backward(nodes, ghosts, edges, send, recv, recv_down, count, w, pre_in, inb, node_ct, edge_ct,
             hid, du, dpre, edge_grad, ghost_grad, grads):
    ef, es, esc, nf, ns, nsc = w
    p = nodes.shape[0]
    ghost_n = ghosts.shape[0]
    blocks = edges.shape[0] // TILE
    ws, wr, we = (ef[i * L:(i + 1) * L, :] for i in range(3))
    nb = nodes[...]
    pre_n = mm(nb, nf[:L, :]) + mm(inb[...], nf[L:, :])
    hid_n, slope_n = silu_parts(pre_n)
    hid_n = hid_n.astype(BF)
    hat, inv = standard(mm(hid_n, ns[...]))
    node_scale_grad = jnp.sum(node_ct * hat, axis=0, keepdims=True)
    du_n = standard_back(node_ct * nsc[...], hat, inv).astype(BF)
    dpre_n = (mm_nt(du_n, ns[...]).astype(BF).astype(F32) * slope_n).astype(BF)
    grads[512:640, :] = mm_tn(nb, dpre_n).astype(BF)
    grads[640:768, :] = mm_tn(inb[...], dpre_n).astype(BF)
    grads[768:896, :] = mm_tn(hid_n, du_n).astype(BF)
    node_grad = node_ct + mm_nt(dpre_n, nf[:L, :])
    dinb = mm_nt(dpre_n, nf[L:, :]).astype(BF)
    tiles = [dinb[t * TILE:(t + 1) * TILE, :] for t in range(p // TILE)]

    def block(tile_grad):
        def body(b, scale_grad):
            rows = rows_of(b)
            pre = pre_in[rows, :]
            h, slope = silu_parts(pre)
            h = h.astype(BF)
            hat, inv = standard(mm(h, es[...]))
            ect = edge_ct[rows, :].astype(F32)
            dm = (ect + mm(picks(recv_down[rows, :], TILE), tile_grad)) * live(count, b)
            scale_grad = scale_grad + jnp.sum(dm * hat, axis=0, keepdims=True)
            d = standard_back(dm * esc[...], hat, inv).astype(BF)
            dp = (mm_nt(d, es[...]) * slope).astype(BF)
            hid[rows, :] = h
            du[rows, :] = d
            dpre[rows, :] = dp
            edge_grad[rows, :] = (ect + mm_nt(dp, we)).astype(edge_grad.dtype)
            return scale_grad
        return body

    scale_grad = jnp.zeros((1, L), F32)
    for t, tile_grad in enumerate(tiles):
        scale_grad = lax.fori_loop(t * DEG, (t + 1) * DEG, block(tile_grad), scale_grad, unroll=4)
    grads[384:512, :] = mm_tn(hid[...], du[...]).astype(BF)
    grads[256:384, :] = mm_tn(edges[...], dpre[...]).astype(BF)
    row = lax.broadcasted_iota(jnp.int32, (16, L), 0)
    scales = jnp.where(row == 0, scale_grad, jnp.where(row == 1, node_scale_grad, 0.0))
    grads[896:912, :] = scales.astype(BF)
    parts = []
    for t in range(p // TILE):
        total = jnp.zeros((TILE, L), F32)
        for j in range(DEG):
            b = t * DEG + j
            at = slice(b * TILE, (b + 1) * TILE)
            total += mm(drops(recv[:, at], 0, TILE), dpre[at, :])
        parts.append(total.astype(BF))
    gr = jnp.concatenate(parts, axis=0)
    grads[L:2 * L, :] = mm_tn(nb, gr).astype(BF)
    node_grad = node_grad + mm_nt(gr, wr)
    ids = table_ids(send[...], p, ghost_n // SLOTS)
    parts = [
        mm(drops(ids, k, L), dpre[...]).astype(BF) for k in range(0, p + ghost_n, L)
    ]
    gs = jnp.concatenate(parts[:p // L], axis=0)
    gg = jnp.concatenate(parts[p // L:], axis=0)
    grads[:L, :] = (mm_tn(nb, gs) + mm_tn(ghosts[...], gg)).astype(BF)
    ghost_grad[...] = mm_nt(gg, ws).astype(BF)
    return node_grad + mm_nt(gs, ws)


def pick_ghosts(nodes, ghost_ids, picked):
    for c in range(SLOTS):
        picked[c * L:(c + 1) * L, :] = mm(
            picks(down(ghost_row(ghost_ids, c)), nodes.shape[0]), nodes[...]
        ).astype(BF)


def put_back(ghost_ids, returned, p):
    ids = jnp.concatenate([ghost_row(ghost_ids, c) for c in range(SLOTS)], axis=1)
    return jnp.concatenate([mm(drops(ids, k, L), returned[...]) for k in range(0, p, L)], axis=0)


def layer_of(i, ef, es, esc, nf, ns, nsc):
    return ef.at[i], es.at[i], esc.at[i:i + 1], nf.at[i], ns.at[i], nsc.at[i:i + 1]


def pick_kernel(nodes, ghost_ids, picked):
    pick_ghosts(nodes, ghost_ids, picked)


def first_kernel(count, nodes, ghosts, edges, send_down, recv, recv_down, ghost_ids, ef, es, esc, nf, ns, nsc,
                 pre, edges_out, inb, nodes_out, picked, table, msg):
    forward(nodes, ghosts, edges, send_down, recv, recv_down, count[0], layer_of(0, ef, es, esc, nf, ns, nsc), table, msg,
            pre, edges_out, inb, nodes_out)
    pick_ghosts(nodes_out, ghost_ids, picked)


def last_kernel(count, nodes, ghosts, edges, send, send_down, recv, recv_down, node_ct, edge_ct, ef, es, esc,
                nf, ns, nsc, edges_out, nodes_out, edge_grad, ghost_grad, grads, node_grad,
                table, msg, pre, inb, hid, du, dpre):
    w = layer_of(1, ef, es, esc, nf, ns, nsc)
    forward(nodes, ghosts, edges, send_down, recv, recv_down, count[0], w, table, msg, pre, edges_out, inb,
            nodes_out)
    node_grad[...] = backward(nodes, ghosts, edges, send, recv, recv_down, count[0], w, pre, inb,
                              node_ct[...].astype(F32), edge_ct, hid, du, dpre, edge_grad,
                              ghost_grad, grads)


def low_kernel(count, nodes, ghosts, edges, send, recv, recv_down, ghost_ids, upper_grad,
               returned, edge_ct, pre, inb, ef, es, esc, nf, ns, nsc,
               edge_grad, ghost_grad, grads, node_grad, hid, du, dpre):
    w = layer_of(0, ef, es, esc, nf, ns, nsc)
    ct = upper_grad[...] + put_back(ghost_ids, returned, nodes.shape[0])
    node_grad[...] = backward(nodes, ghosts, edges, send, recv, recv_down, count[0], w, pre, inb,
                              ct.astype(BF).astype(F32), edge_ct, hid, du, dpre, edge_grad,
                              ghost_grad, grads)


def neighbours(gx, gy):
    x, y = lax.axis_index("gx"), lax.axis_index("gy")
    found = []
    for dx, dy in OFFSETS:
        there = (x + dx >= 0) & (x + dx < gx) & (y + dy >= 0) & (y + dy < gy)
        found.append((there, (lax.rem(x + dx + gx, gx), lax.rem(y + dy + gy, gy))))
    return found


def swap(found, src, dst, send_sem, recv_sem):
    copies = [
        pltpu.make_async_remote_copy(
            src_ref=src.at[c],
            dst_ref=dst.at[SLOTS - 1 - c],
            send_sem=send_sem.at[c],
            recv_sem=recv_sem.at[SLOTS - 1 - c],
            device_id=place,
            device_id_type=MESH,
        )
        for c, (_, place) in enumerate(found)
    ]
    for (there, _), copy in zip(found, copies):
        pl.when(there)(copy.start)
    return copies


def finish_swap(found, copies, src, dst, send_sem, recv_sem):
    for c, ((there, place), copy) in enumerate(zip(found, copies)):
        pl.when(there)(copy.wait_send)
        arrival = pltpu.make_async_remote_copy(
            src_ref=src.at[c], dst_ref=dst.at[c], send_sem=send_sem.at[c],
            recv_sem=recv_sem.at[c], device_id=place, device_id_type=MESH,
        )
        pl.when(there)(arrival.wait_recv)


def first_swap_kernel(gx, gy, p, src, send, recv, dst, send_down, recv_down, send_sem, recv_sem):
    def columns():
        ids = table_ids(send[...], p, src.shape[1])
        for i in range(0, send.shape[1], TILE):
            send_down[i:i + TILE, :] = down(ids[:, i:i + TILE])
            recv_down[i:i + TILE, :] = down(recv[:, i:i + TILE])

    swap_kernel(gx, gy, src, dst, send_sem, recv_sem, columns)


def swap_kernel(gx, gy, src, dst, send_sem, recv_sem, beside=None):
    found = neighbours(gx, gy)
    barrier = pltpu.get_barrier_semaphore()
    for there, place in found:
        @pl.when(there)
        def _():
            pl.semaphore_signal(barrier, inc=1, device_id=place, device_id_type=MESH)
    for c, (there, _) in enumerate(found):
        @pl.when(jnp.logical_not(there))
        def _():
            dst[c] = jnp.zeros(dst.shape[1:], dst.dtype)
    peers = sum(jnp.where(there, 1, 0) for there, _ in found)
    pl.semaphore_wait(barrier, peers)
    copies = swap(found, src, dst, send_sem, recv_sem)
    if beside is not None:
        beside()
    finish_swap(found, copies, src, dst, send_sem, recv_sem)


def reduce_kernel(gx, gy, rows, src, grads0, grads1, dst, total, packed, half, part, got_core,
                  got_x, got_gx, send_sem, recv_sem):
    x, y = lax.axis_index("gx"), lax.axis_index("gy")
    core, chip = lax.rem(y, 2), y // 2
    chips = gy // 2
    found = neighbours(gx, gy)
    keep = [rows // 2, rows // (2 * chips), rows // (2 * chips * gx)]
    start = [0, core * keep[0], core * keep[0] + chip * keep[1]]
    groups = [
        (2, core, lambda j: (x, chip * 2 + j)),
        (chips, chip, lambda j: (x, j * 2 + core)),
        (gx, x, lambda j: (j, y)),
    ]
    barrier = pltpu.get_barrier_semaphore()
    for there, place in found:
        @pl.when(there)
        def _():
            pl.semaphore_signal(barrier, inc=1, device_id=place, device_id_type=MESH)
    peers = sum(jnp.where(there, 1, 0) for there, _ in found)
    for count, me, place in groups:
        for d in range(1, count):
            pl.semaphore_signal(barrier, inc=1, device_id=place(lax.rem(me + d, count)),
                                device_id_type=MESH)
            peers = peers + 1
    for c, (there, _) in enumerate(found):
        @pl.when(jnp.logical_not(there))
        def _():
            dst[c] = jnp.zeros(dst.shape[1:], dst.dtype)
    n = grads0.shape[0]
    packed[:n, :] = grads0[...]
    packed[n:2 * n, :] = grads1[...]
    packed[2 * n:, :] = jnp.zeros((rows - 2 * n, L), BF)
    pl.semaphore_wait(barrier, peers)
    swaps = swap(found, src, dst, send_sem, recv_sem)

    def at(index, size):
        return pl.ds(pl.multiple_of(index, 16), size)

    sent = []
    sem = SLOTS
    held = packed
    for (count, me, place), size, got, out in zip(
        groups, keep, (got_core, got_x, got_gx), (half, part, total)
    ):
        copies = []
        for d in range(1, count):
            peer = lax.rem(me + d, count)
            copies.append(pltpu.make_async_remote_copy(
                src_ref=held.at[at(peer * size, size)], dst_ref=got.at[d - 1],
                send_sem=send_sem.at[sem], recv_sem=recv_sem.at[sem],
                device_id=place(peer), device_id_type=MESH,
            ))
            sem += 1
            copies[-1].start()
        mine = held[at(me * size, size), :].astype(F32)
        for d, copy in enumerate(copies):
            copy.wait_recv()
            mine = mine + got[d].astype(F32)
        if out is total:
            out[at(start[2] + x * size, size), :] = mine.astype(BF)
        else:
            out[...] = mine.astype(BF)
        sent += copies
        held = out
    for (count, me, place), size, first in reversed(list(zip(groups, keep, start))):
        copies = []
        own = total.at[at(first + me * size, size)]
        for d in range(1, count):
            copies.append(pltpu.make_async_remote_copy(
                src_ref=own, dst_ref=own, send_sem=send_sem.at[sem], recv_sem=recv_sem.at[sem],
                device_id=place(lax.rem(me + d, count)), device_id_type=MESH,
            ))
            copies[-1].start()
            origin = lax.rem(me - d + count, count)
            block = total.at[at(first + origin * size, size)]
            copies.append(pltpu.make_async_remote_copy(
                src_ref=block, dst_ref=block, send_sem=send_sem.at[sem], recv_sem=recv_sem.at[sem],
                device_id=place(origin), device_id_type=MESH,
            ))
            sem += 1
        for copy in copies[1::2]:
            copy.wait_recv()
        sent += copies[::2]
    for copy in sent:
        copy.wait_send()
    finish_swap(found, swaps, src, dst, send_sem, recv_sem)


def end_kernel(ghost_ids, lower, returned, total, node_grad, ef, es, esc, nf, ns, nsc):
    p = lower.shape[0]
    node_grad[...] = lower[...] + put_back(ghost_ids, returned, p)
    for i in range(LAYERS):
        base = i * 912
        for out, first, last in ((ef, 0, 384), (es, 384, 512), (nf, 512, 768), (ns, 768, 896)):
            out[i] = total[base + first:base + last, :].astype(F32)
        scales = total[base + 896:base + 912, :].astype(F32)
        esc[i:i + 1, :] = scales[:1, :]
        nsc[i:i + 1, :] = scales[1:2, :]


def solution(mesh):
    gx, gy = mesh.shape["gx"], mesh.shape["gy"]

    def call(kernel, mib, giga, shapes, scratch, args, smem_first=True, **params):
        return pl.pallas_call(
            kernel,
            out_shape=shapes,
            in_specs=[SMEM if smem_first and i == 0 else VMEM for i in range(len(args))],
            out_specs=jax.tree.map(lambda _: VMEM, shapes),
            scratch_shapes=scratch,
            cost_estimate=pl.CostEstimate(
                flops=giga * 10**9, bytes_accessed=giga * 2**21, transcendentals=0
            ),
            compiler_params=pltpu.CompilerParams(vmem_limit_bytes=mib * 2**20, **params),
        )(*args)

    swap_sems = [pltpu.SemaphoreType.DMA((SLOTS,)), pltpu.SemaphoreType.DMA((SLOTS,))]

    def exchange(value, collective_id):
        shape = (SLOTS, value.shape[0] // SLOTS, L)
        out = call(
            functools.partial(swap_kernel, gx, gy),
            4,
            7,
            jax.ShapeDtypeStruct(shape, BF),
            swap_sems,
            (value.reshape(shape),),
            smem_first=False,
            collective_id=collective_id,
            has_side_effects=True,
        )
        return out.reshape(value.shape)

    def on_device(latents, edge_latents, senders, receivers, ghost_rows, edge_count,
                  node_cotangent, edge_cotangent, edge_first, edge_second, edge_scale,
                  node_first, node_second, node_scale):
        nodes, edges = latents[0, 0], edge_latents[0, 0]
        p, e = nodes.shape[0], edges.shape[0]
        ghost_n = SLOTS * ghost_rows.shape[-1]
        send, recv = senders.reshape(1, e), receivers.reshape(1, e)
        count = edge_count.reshape(1)
        weights = (edge_first, edge_second, edge_scale, node_first, node_second, node_scale)

        def s(shape, dtype):
            return jax.ShapeDtypeStruct(shape, dtype)

        back_scratch = [pltpu.VMEM((e, L), BF)] * 3
        fore_scratch = [pltpu.VMEM((p + ghost_n + TILE + L, L), BF), pltpu.VMEM((e, L), BF)]
        n = 912
        grad_rows = s((n, L), BF)

        picked = call(pick_kernel, 8, 1, s((ghost_n, L), BF), [], (nodes, ghost_rows), smem_first=False)
        slots = (SLOTS, ghost_n // SLOTS, L)
        ghosts0, send_down, recv_down = call(
            functools.partial(first_swap_kernel, gx, gy, p),
            8,
            7,
            (s(slots, BF), s((e, L), I16), s((e, L), I16)),
            swap_sems,
            (picked.reshape(slots), send, recv),
            smem_first=False,
            collective_id=0,
            has_side_effects=True,
        )
        ghosts0 = ghosts0.reshape(ghost_n, L)
        pre0, edges1, inb0, nodes1, picked1 = call(
            first_kernel,
            24,
            10,
            (s((e, L), F32), s((e, L), BF), s((p, L), BF), s((p, L), BF), s((ghost_n, L), BF)),
            fore_scratch,
            (count, nodes, ghosts0, edges, send_down, recv, recv_down, ghost_rows, *weights),
        )
        ghosts1 = exchange(picked1, 1)
        edges_out, nodes_out, edge_ct, ghost_ct, grads1, upper = call(
            last_kernel,
            32,
            22,
            (s((e, L), BF), s((p, L), BF), s((e, L), BF), s((ghost_n, L), BF), grad_rows,
             s((p, L), F32)),
            fore_scratch + [pltpu.VMEM((e, L), F32), pltpu.VMEM((p, L), BF)] + back_scratch,
            (count, nodes1, ghosts1, edges1, send, send_down, recv, recv_down, node_cotangent[0, 0],
             edge_cotangent[0, 0], *weights),
        )
        returned1 = exchange(ghost_ct, 2)
        edge_grad, ghost_ct0, grads0, lower = call(
            low_kernel,
            28,
            15,
            (s((e, L), F32), s((ghost_n, L), BF), grad_rows, s((p, L), F32)),
            back_scratch,
            (count, nodes, ghosts0, edges, send, recv, recv_down, ghost_rows, upper, returned1,
             edge_ct, pre0, inb0, *weights),
        )
        unit = 16 * gx * gy
        rows = -(-2 * n // unit) * unit
        chips = gy // 2
        quarter = rows // (2 * chips)
        sems = SLOTS + 2 * (1 + chips - 1 + gx - 1)
        returned0, total = call(
            functools.partial(reduce_kernel, gx, gy, rows),
            12,
            20,
            (s(slots, BF), s((rows, L), BF)),
            [pltpu.VMEM((rows, L), BF), pltpu.VMEM((rows // 2, L), BF), pltpu.VMEM((quarter, L), BF),
             pltpu.VMEM((1, rows // 2, L), BF), pltpu.VMEM((chips - 1, quarter, L), BF),
             pltpu.VMEM((gx - 1, quarter // gx, L), BF),
             pltpu.SemaphoreType.DMA((sems,)), pltpu.SemaphoreType.DMA((sems,))],
            (ghost_ct0.reshape(slots), grads0, grads1),
            smem_first=False,
            collective_id=3,
            has_side_effects=True,
        )
        node_grad, *weight_grads = call(
            end_kernel,
            12,
            1,
            (s((p, L), F32),) + tuple(s(w.shape, F32) for w in weights),
            [],
            (ghost_rows, lower, returned0.reshape(ghost_n, L), total),
            smem_first=False,
        )
        return (
            nodes_out[None, None],
            edges_out[None, None],
            node_grad[None, None],
            edge_grad[None, None],
            *weight_grads,
        )

    cell = P("gx", "gy", None, None)
    line = P("gx", "gy", None)
    return jax.shard_map(
        on_device,
        mesh=mesh,
        in_specs=(cell, cell, line, line, P("gx", "gy", None, None, None), P("gx", "gy"), cell,
                  cell) + (P(),) * 6,
        out_specs=(cell,) * 4 + (P(),) * 6,
        check_vma=False,
    )
```

```python
import functools

import jax
import jax.numpy as jnp
from jax import lax
from jax.experimental import pallas as pl
from jax.experimental.pallas import tpu as pltpu
from jax.sharding import PartitionSpec as P

L = 128
LAYERS = 2
TILE = 256
DEG = 8
SPAN = TILE * DEG
EPS = 1e-05
MESH = pl.DeviceIdType.MESH
F32 = jnp.float32
BF = jnp.bfloat16
I16 = jnp.int16
VMEM = pl.BlockSpec(memory_space=pltpu.VMEM)
SMEM = pl.BlockSpec(memory_space=pltpu.SMEM)
OFFSETS = [(a - 1, b - 1) for a in range(3) for b in range(3) if (a, b) != (1, 1)]
SLOTS = len(OFFSETS)


def mm(a, b):
    return jnp.dot(a, b, preferred_element_type=F32)


def mm_nt(a, b):
    return lax.dot_general(a, b, (((1,), (1,)), ((), ())), preferred_element_type=F32)


def mm_tn(a, b):
    return lax.dot_general(a, b, (((0,), (0,)), ((), ())), preferred_element_type=F32)


def hot(mask):
    return jnp.where(mask, jnp.ones((), BF), jnp.zeros((), BF))


def down(ids_row, width=L):
    n = ids_row.shape[1]
    return jnp.broadcast_to(ids_row, (L, n)).T.astype(I16)


def picks(column, size):
    lane = lax.broadcasted_iota(jnp.int32, column.shape, 1).astype(I16)
    return jnp.concatenate([hot(column == lane + jnp.int16(k)) for k in range(0, size, L)], axis=1)


def drops(ids_row, first, size):
    shape = (size, ids_row.shape[1])
    row = lax.broadcasted_iota(jnp.int32, shape, 0) + first
    return hot(row.astype(I16) == jnp.broadcast_to(ids_row, shape).astype(I16))


def silu(v):
    return v / (1.0 + jnp.exp(-v))


def silu_parts(v):
    s = 1.0 / (1.0 + jnp.exp(-v))
    return v * s, s * (1.0 + v * (1.0 - s))


def lane_mean(v):
    high = v.astype(BF)
    low = (v - high.astype(F32)).astype(BF)
    return mm(jnp.concatenate([high, low], axis=1), jnp.full((2 * L, L), 1.0 / L, BF))


def standard(v):
    center = lane_mean(v)
    off = v - center
    inv = lax.rsqrt(lane_mean(off * off) + EPS)
    return off * inv, inv


def standard_back(g, hat, inv):
    a = lane_mean(g)
    b = lane_mean(g * hat)
    return inv * (g - a - hat * b)


def live(count, b):
    row = lax.broadcasted_iota(jnp.int32, (TILE, L), 0) + b * TILE
    return jnp.where(row < count, 1.0, 0.0)


def rows_of(b):
    return pl.ds(pl.multiple_of(b * TILE, TILE), TILE)


def table_ids(ids, p, g):
    return jnp.where(ids >= p + 4 * g, ids - g, ids)


def ghost_row(ghost_ids, c):
    a, b = divmod(c + (c >= 4), 3)
    return ghost_ids[0, 0, a, b:b + 1, :]


def forward(nodes, ghosts, edges, send_down, recv, recv_down, count, w, table, msg, pre_out, edges_out,
            inb_out, nodes_out):
    ef, es, esc, nf, ns, nsc = w
    p = nodes.shape[0]
    size = p + ghosts.shape[0]
    ws, wr, we = (ef[i * L:(i + 1) * L, :] for i in range(3))
    table[:p, :] = mm(nodes[...], ws).astype(BF)
    table[p:size, :] = mm(ghosts[...], ws).astype(BF)
    table[size + TILE:size + TILE + L, :] = we

    def block(b, carry):
        rows = rows_of(b)
        left = jnp.concatenate(
            [
                picks(send_down[rows, :], size),
                picks(recv_down[rows, :], TILE),
                edges[rows, :],
            ],
            axis=1,
        )
        pre = mm(left, table[...])
        pre_out[rows, :] = pre
        hat, _ = standard(mm(silu(pre).astype(BF), es[...]))
        message = hat * esc[...] * live(count, b)
        edges_out[rows, :] = (edges[rows, :].astype(F32) + message).astype(BF)
        msg[rows, :] = message.astype(BF)
        return carry

    for t in range(p // TILE):
        table[size:size + TILE, :] = mm(nodes[t * TILE:(t + 1) * TILE, :], wr).astype(BF)
        lax.fori_loop(t * DEG, (t + 1) * DEG, block, 0, unroll=4)
    for t in range(p // TILE):
        total = jnp.zeros((TILE, L), F32)
        for j in range(DEG):
            b = t * DEG + j
            at = slice(b * TILE, (b + 1) * TILE)
            total += mm(drops(recv[:, at], 0, TILE), msg[at, :])
        inb_out[t * TILE:(t + 1) * TILE, :] = total.astype(BF)
    pre_n = mm(nodes[...], nf[:L, :]) + mm(inb_out[...], nf[L:, :])
    hat, _ = standard(mm(silu(pre_n).astype(BF), ns[...]))
    nodes_out[...] = (nodes[...].astype(F32) + hat * nsc[...]).astype(BF)


def backward(nodes, ghosts, edges, send, recv, recv_down, count, w, pre_in, inb, node_ct, edge_ct,
             hid, du, dpre, edge_grad, ghost_grad, grads):
    ef, es, esc, nf, ns, nsc = w
    p = nodes.shape[0]
    ghost_n = ghosts.shape[0]
    blocks = edges.shape[0] // TILE
    ws, wr, we = (ef[i * L:(i + 1) * L, :] for i in range(3))
    nb = nodes[...]
    pre_n = mm(nb, nf[:L, :]) + mm(inb[...], nf[L:, :])
    hid_n, slope_n = silu_parts(pre_n)
    hid_n = hid_n.astype(BF)
    hat, inv = standard(mm(hid_n, ns[...]))
    node_scale_grad = jnp.sum(node_ct * hat, axis=0, keepdims=True)
    du_n = standard_back(node_ct * nsc[...], hat, inv).astype(BF)
    dpre_n = (mm_nt(du_n, ns[...]).astype(BF).astype(F32) * slope_n).astype(BF)
    grads[512:640, :] = mm_tn(nb, dpre_n).astype(BF)
    grads[640:768, :] = mm_tn(inb[...], dpre_n).astype(BF)
    grads[768:896, :] = mm_tn(hid_n, du_n).astype(BF)
    node_grad = node_ct + mm_nt(dpre_n, nf[:L, :])
    dinb = mm_nt(dpre_n, nf[L:, :]).astype(BF)
    tiles = [dinb[t * TILE:(t + 1) * TILE, :] for t in range(p // TILE)]

    def block(tile_grad):
        def body(b, scale_grad):
            rows = rows_of(b)
            pre = pre_in[rows, :]
            h, slope = silu_parts(pre)
            h = h.astype(BF)
            hat, inv = standard(mm(h, es[...]))
            ect = edge_ct[rows, :].astype(F32)
            dm = (ect + mm(picks(recv_down[rows, :], TILE), tile_grad)) * live(count, b)
            scale_grad = scale_grad + jnp.sum(dm * hat, axis=0, keepdims=True)
            d = standard_back(dm * esc[...], hat, inv).astype(BF)
            dp = (mm_nt(d, es[...]) * slope).astype(BF)
            hid[rows, :] = h
            du[rows, :] = d
            dpre[rows, :] = dp
            edge_grad[rows, :] = (ect + mm_nt(dp, we)).astype(edge_grad.dtype)
            return scale_grad
        return body

    scale_grad = jnp.zeros((1, L), F32)
    for t, tile_grad in enumerate(tiles):
        scale_grad = lax.fori_loop(t * DEG, (t + 1) * DEG, block(tile_grad), scale_grad, unroll=4)
    grads[384:512, :] = mm_tn(hid[...], du[...]).astype(BF)
    grads[256:384, :] = mm_tn(edges[...], dpre[...]).astype(BF)
    row = lax.broadcasted_iota(jnp.int32, (16, L), 0)
    scales = jnp.where(row == 0, scale_grad, jnp.where(row == 1, node_scale_grad, 0.0))
    grads[896:912, :] = scales.astype(BF)
    parts = []
    for t in range(p // TILE):
        total = jnp.zeros((TILE, L), F32)
        for j in range(DEG):
            b = t * DEG + j
            at = slice(b * TILE, (b + 1) * TILE)
            total += mm(drops(recv[:, at], 0, TILE), dpre[at, :])
        parts.append(total.astype(BF))
    gr = jnp.concatenate(parts, axis=0)
    grads[L:2 * L, :] = mm_tn(nb, gr).astype(BF)
    node_grad = node_grad + mm_nt(gr, wr)
    ids = table_ids(send[...], p, ghost_n // SLOTS)
    parts = [
        mm(drops(ids, k, L), dpre[...]).astype(BF) for k in range(0, p + ghost_n, L)
    ]
    gs = jnp.concatenate(parts[:p // L], axis=0)
    gg = jnp.concatenate(parts[p // L:], axis=0)
    grads[:L, :] = (mm_tn(nb, gs) + mm_tn(ghosts[...], gg)).astype(BF)
    ghost_grad[...] = mm_nt(gg, ws).astype(BF)
    return node_grad + mm_nt(gs, ws)


def pick_ghosts(nodes, ghost_ids, picked):
    for c in range(SLOTS):
        picked[c * L:(c + 1) * L, :] = mm(
            picks(down(ghost_row(ghost_ids, c)), nodes.shape[0]), nodes[...]
        ).astype(BF)


def put_back(ghost_ids, returned, p):
    ids = jnp.concatenate([ghost_row(ghost_ids, c) for c in range(SLOTS)], axis=1)
    return jnp.concatenate([mm(drops(ids, k, L), returned[...]) for k in range(0, p, L)], axis=0)


def layer_of(i, ef, es, esc, nf, ns, nsc):
    return ef.at[i], es.at[i], esc.at[i:i + 1], nf.at[i], ns.at[i], nsc.at[i:i + 1]


def pick_kernel(nodes, ghost_ids, picked):
    pick_ghosts(nodes, ghost_ids, picked)


def first_kernel(count, nodes, ghosts, edges, send_down, recv, recv_down, ghost_ids, ef, es, esc, nf, ns, nsc,
                 pre, edges_out, inb, nodes_out, picked, table, msg):
    forward(nodes, ghosts, edges, send_down, recv, recv_down, count[0], layer_of(0, ef, es, esc, nf, ns, nsc), table, msg,
            pre, edges_out, inb, nodes_out)
    pick_ghosts(nodes_out, ghost_ids, picked)


def last_kernel(count, nodes, ghosts, edges, send, send_down, recv, recv_down, node_ct, edge_ct, ef, es, esc,
                nf, ns, nsc, edges_out, nodes_out, edge_grad, ghost_grad, grads, node_grad,
                table, msg, pre, inb, hid, du, dpre):
    w = layer_of(1, ef, es, esc, nf, ns, nsc)
    forward(nodes, ghosts, edges, send_down, recv, recv_down, count[0], w, table, msg, pre, edges_out, inb,
            nodes_out)
    node_grad[...] = backward(nodes, ghosts, edges, send, recv, recv_down, count[0], w, pre, inb,
                              node_ct[...].astype(F32), edge_ct, hid, du, dpre, edge_grad,
                              ghost_grad, grads)


def low_kernel(count, nodes, ghosts, edges, send, recv, recv_down, ghost_ids, upper_grad,
               returned, edge_ct, pre, inb, ef, es, esc, nf, ns, nsc,
               edge_grad, ghost_grad, grads, node_grad, hid, du, dpre):
    w = layer_of(0, ef, es, esc, nf, ns, nsc)
    ct = upper_grad[...] + put_back(ghost_ids, returned, nodes.shape[0])
    node_grad[...] = backward(nodes, ghosts, edges, send, recv, recv_down, count[0], w, pre, inb,
                              ct.astype(BF).astype(F32), edge_ct, hid, du, dpre, edge_grad,
                              ghost_grad, grads)


def neighbours(gx, gy):
    x, y = lax.axis_index("gx"), lax.axis_index("gy")
    found = []
    for dx, dy in OFFSETS:
        there = (x + dx >= 0) & (x + dx < gx) & (y + dy >= 0) & (y + dy < gy)
        found.append((there, (lax.rem(x + dx + gx, gx), lax.rem(y + dy + gy, gy))))
    return found


def swap(found, src, dst, send_sem, recv_sem):
    copies = [
        pltpu.make_async_remote_copy(
            src_ref=src.at[c],
            dst_ref=dst.at[SLOTS - 1 - c],
            send_sem=send_sem.at[c],
            recv_sem=recv_sem.at[SLOTS - 1 - c],
            device_id=place,
            device_id_type=MESH,
        )
        for c, (_, place) in enumerate(found)
    ]
    for (there, _), copy in zip(found, copies):
        pl.when(there)(copy.start)
    return copies


def finish_swap(found, copies, src, dst, send_sem, recv_sem):
    for c, ((there, place), copy) in enumerate(zip(found, copies)):
        pl.when(there)(copy.wait_send)
        arrival = pltpu.make_async_remote_copy(
            src_ref=src.at[c], dst_ref=dst.at[c], send_sem=send_sem.at[c],
            recv_sem=recv_sem.at[c], device_id=place, device_id_type=MESH,
        )
        pl.when(there)(arrival.wait_recv)


def first_swap_kernel(gx, gy, p, src, send, recv, dst, send_down, recv_down, send_sem, recv_sem):
    def columns():
        ids = table_ids(send[...], p, src.shape[1])
        for i in range(0, send.shape[1], TILE):
            send_down[i:i + TILE, :] = down(ids[:, i:i + TILE])
            recv_down[i:i + TILE, :] = down(recv[:, i:i + TILE])

    swap_kernel(gx, gy, src, dst, send_sem, recv_sem, columns)


def swap_kernel(gx, gy, src, dst, send_sem, recv_sem, beside=None):
    found = neighbours(gx, gy)
    barrier = pltpu.get_barrier_semaphore()
    for there, place in found:
        @pl.when(there)
        def _():
            pl.semaphore_signal(barrier, inc=1, device_id=place, device_id_type=MESH)
    for c, (there, _) in enumerate(found):
        @pl.when(jnp.logical_not(there))
        def _():
            dst[c] = jnp.zeros(dst.shape[1:], dst.dtype)
    peers = sum(jnp.where(there, 1, 0) for there, _ in found)
    pl.semaphore_wait(barrier, peers)
    copies = swap(found, src, dst, send_sem, recv_sem)
    if beside is not None:
        beside()
    finish_swap(found, copies, src, dst, send_sem, recv_sem)


def reduce_kernel(gx, gy, rows, src, grads0, grads1, dst, total, packed, half, part, got_core,
                  got_x, got_gx, send_sem, recv_sem):
    x, y = lax.axis_index("gx"), lax.axis_index("gy")
    core, chip = lax.rem(y, 2), y // 2
    chips = gy // 2
    found = neighbours(gx, gy)
    keep = [rows // 2, rows // (2 * chips), rows // (2 * chips * gx)]
    start = [0, core * keep[0], core * keep[0] + chip * keep[1]]
    groups = [
        (2, core, lambda j: (x, chip * 2 + j)),
        (chips, chip, lambda j: (x, j * 2 + core)),
        (gx, x, lambda j: (j, y)),
    ]
    barrier = pltpu.get_barrier_semaphore()
    for there, place in found:
        @pl.when(there)
        def _():
            pl.semaphore_signal(barrier, inc=1, device_id=place, device_id_type=MESH)
    peers = sum(jnp.where(there, 1, 0) for there, _ in found)
    for count, me, place in groups:
        for d in range(1, count):
            pl.semaphore_signal(barrier, inc=1, device_id=place(lax.rem(me + d, count)),
                                device_id_type=MESH)
            peers = peers + 1
    for c, (there, _) in enumerate(found):
        @pl.when(jnp.logical_not(there))
        def _():
            dst[c] = jnp.zeros(dst.shape[1:], dst.dtype)
    n = grads0.shape[0]
    packed[:n, :] = grads0[...]
    packed[n:2 * n, :] = grads1[...]
    packed[2 * n:, :] = jnp.zeros((rows - 2 * n, L), BF)
    pl.semaphore_wait(barrier, peers)
    swaps = swap(found, src, dst, send_sem, recv_sem)

    def at(index, size):
        return pl.ds(pl.multiple_of(index, 16), size)

    sent = []
    sem = SLOTS
    held = packed
    for (count, me, place), size, got, out in zip(
        groups, keep, (got_core, got_x, got_gx), (half, part, total)
    ):
        copies = []
        for d in range(1, count):
            peer = lax.rem(me + d, count)
            copies.append(pltpu.make_async_remote_copy(
                src_ref=held.at[at(peer * size, size)], dst_ref=got.at[d - 1],
                send_sem=send_sem.at[sem], recv_sem=recv_sem.at[sem],
                device_id=place(peer), device_id_type=MESH,
            ))
            sem += 1
            copies[-1].start()
        mine = held[at(me * size, size), :].astype(F32)
        for d, copy in enumerate(copies):
            copy.wait_recv()
            mine = mine + got[d].astype(F32)
        if out is total:
            out[at(start[2] + x * size, size), :] = mine.astype(BF)
        else:
            out[...] = mine.astype(BF)
        sent += copies
        held = out
    for (count, me, place), size, first in reversed(list(zip(groups, keep, start))):
        copies = []
        own = total.at[at(first + me * size, size)]
        for d in range(1, count):
            copies.append(pltpu.make_async_remote_copy(
                src_ref=own, dst_ref=own, send_sem=send_sem.at[sem], recv_sem=recv_sem.at[sem],
                device_id=place(lax.rem(me + d, count)), device_id_type=MESH,
            ))
            copies[-1].start()
            origin = lax.rem(me - d + count, count)
            block = total.at[at(first + origin * size, size)]
            copies.append(pltpu.make_async_remote_copy(
                src_ref=block, dst_ref=block, send_sem=send_sem.at[sem], recv_sem=recv_sem.at[sem],
                device_id=place(origin), device_id_type=MESH,
            ))
            sem += 1
        for copy in copies[1::2]:
            copy.wait_recv()
        sent += copies[::2]
    for copy in sent:
        copy.wait_send()
    finish_swap(found, swaps, src, dst, send_sem, recv_sem)


def end_kernel(ghost_ids, lower, returned, total, node_grad, ef, es, esc, nf, ns, nsc):
    p = lower.shape[0]
    node_grad[...] = lower[...] + put_back(ghost_ids, returned, p)
    for i in range(LAYERS):
        base = i * 912
        for out, first, last in ((ef, 0, 384), (es, 384, 512), (nf, 512, 768), (ns, 768, 896)):
            out[i] = total[base + first:base + last, :].astype(F32)
        scales = total[base + 896:base + 912, :].astype(F32)
        esc[i:i + 1, :] = scales[:1, :]
        nsc[i:i + 1, :] = scales[1:2, :]


def solution(mesh):
    gx, gy = mesh.shape["gx"], mesh.shape["gy"]

    def call(kernel, mib, giga, shapes, scratch, args, smem_first=True, **params):
        return pl.pallas_call(
            kernel,
            out_shape=shapes,
            in_specs=[SMEM if smem_first and i == 0 else VMEM for i in range(len(args))],
            out_specs=jax.tree.map(lambda _: VMEM, shapes),
            scratch_shapes=scratch,
            cost_estimate=pl.CostEstimate(
                flops=giga * 10**9, bytes_accessed=giga * 2**21, transcendentals=0
            ),
            compiler_params=pltpu.CompilerParams(vmem_limit_bytes=mib * 2**20, **params),
        )(*args)

    swap_sems = [pltpu.SemaphoreType.DMA((SLOTS,)), pltpu.SemaphoreType.DMA((SLOTS,))]

    def exchange(value, collective_id):
        shape = (SLOTS, value.shape[0] // SLOTS, L)
        out = call(
            functools.partial(swap_kernel, gx, gy),
            4,
            7,
            jax.ShapeDtypeStruct(shape, BF),
            swap_sems,
            (value.reshape(shape),),
            smem_first=False,
            collective_id=collective_id,
            has_side_effects=True,
        )
        return out.reshape(value.shape)

    def on_device(latents, edge_latents, senders, receivers, ghost_rows, edge_count,
                  node_cotangent, edge_cotangent, edge_first, edge_second, edge_scale,
                  node_first, node_second, node_scale):
        nodes, edges = latents[0, 0], edge_latents[0, 0]
        p, e = nodes.shape[0], edges.shape[0]
        ghost_n = SLOTS * ghost_rows.shape[-1]
        send, recv = senders.reshape(1, e), receivers.reshape(1, e)
        count = edge_count.reshape(1)
        weights = (edge_first, edge_second, edge_scale, node_first, node_second, node_scale)

        def s(shape, dtype):
            return jax.ShapeDtypeStruct(shape, dtype)

        back_scratch = [pltpu.VMEM((e, L), BF)] * 3
        fore_scratch = [pltpu.VMEM((p + ghost_n + TILE + L, L), BF), pltpu.VMEM((e, L), BF)]
        n = 912
        grad_rows = s((n, L), BF)

        picked = call(pick_kernel, 8, 1, s((ghost_n, L), BF), [], (nodes, ghost_rows), smem_first=False)
        slots = (SLOTS, ghost_n // SLOTS, L)
        ghosts0, send_down, recv_down = call(
            functools.partial(first_swap_kernel, gx, gy, p),
            8,
            7,
            (s(slots, BF), s((e, L), I16), s((e, L), I16)),
            swap_sems,
            (picked.reshape(slots), send, recv),
            smem_first=False,
            collective_id=0,
            has_side_effects=True,
        )
        ghosts0 = ghosts0.reshape(ghost_n, L)
        pre0, edges1, inb0, nodes1, picked1 = call(
            first_kernel,
            24,
            10,
            (s((e, L), F32), s((e, L), BF), s((p, L), BF), s((p, L), BF), s((ghost_n, L), BF)),
            fore_scratch,
            (count, nodes, ghosts0, edges, send_down, recv, recv_down, ghost_rows, *weights),
        )
        ghosts1 = exchange(picked1, 1)
        edges_out, nodes_out, edge_ct, ghost_ct, grads1, upper = call(
            last_kernel,
            32,
            22,
            (s((e, L), BF), s((p, L), BF), s((e, L), BF), s((ghost_n, L), BF), grad_rows,
             s((p, L), F32)),
            fore_scratch + [pltpu.VMEM((e, L), F32), pltpu.VMEM((p, L), BF)] + back_scratch,
            (count, nodes1, ghosts1, edges1, send, send_down, recv, recv_down, node_cotangent[0, 0],
             edge_cotangent[0, 0], *weights),
        )
        returned1 = exchange(ghost_ct, 2)
        edge_grad, ghost_ct0, grads0, lower = call(
            low_kernel,
            28,
            15,
            (s((e, L), F32), s((ghost_n, L), BF), grad_rows, s((p, L), F32)),
            back_scratch,
            (count, nodes, ghosts0, edges, send, recv, recv_down, ghost_rows, upper, returned1,
             edge_ct, pre0, inb0, *weights),
        )
        unit = 16 * gx * gy
        rows = -(-2 * n // unit) * unit
        chips = gy // 2
        quarter = rows // (2 * chips)
        sems = SLOTS + 2 * (1 + chips - 1 + gx - 1)
        returned0, total = call(
            functools.partial(reduce_kernel, gx, gy, rows),
            12,
            20,
            (s(slots, BF), s((rows, L), BF)),
            [pltpu.VMEM((rows, L), BF), pltpu.VMEM((rows // 2, L), BF), pltpu.VMEM((quarter, L), BF),
             pltpu.VMEM((1, rows // 2, L), BF), pltpu.VMEM((chips - 1, quarter, L), BF),
             pltpu.VMEM((gx - 1, quarter // gx, L), BF),
             pltpu.SemaphoreType.DMA((sems,)), pltpu.SemaphoreType.DMA((sems,))],
            (ghost_ct0.reshape(slots), grads0, grads1),
            smem_first=False,
            collective_id=3,
            has_side_effects=True,
        )
        node_grad, *weight_grads = call(
            end_kernel,
            12,
            1,
            (s((p, L), F32),) + tuple(s(w.shape, F32) for w in weights),
            [],
            (ghost_rows, lower, returned0.reshape(ghost_n, L), total),
            smem_first=False,
        )
        return (
            nodes_out[None, None],
            edges_out[None, None],
            node_grad[None, None],
            edge_grad[None, None],
            *weight_grads,
        )

    cell = P("gx", "gy", None, None)
    line = P("gx", "gy", None)
    return jax.shard_map(
        on_device,
        mesh=mesh,
        in_specs=(cell, cell, line, line, P("gx", "gy", None, None, None), P("gx", "gy"), cell,
                  cell) + (P(),) * 6,
        out_specs=(cell,) * 4 + (P(),) * 6,
        check_vma=False,
    )
```
